32 devices in a mesh: dp: 4 (over x, core), mp: 8 (over z, y).
Axes of the slice: x: 2, y: 2, z: 4, core: 2. Of those that a mesh axis runs over, the one named last changes fastest.
Arguments:
- accumulated: bfloat16 [16384, 28672], P('dp', 'mp'), may hold values from -6 to 6
- signs: int32 [8192], replicated, may hold values from 0 to 1
- q_start: bfloat16 [28672, 128], P('mp'), may hold values from -6 to 6
Outputs:
- new_error: bfloat16 [16384, 28672], P('dp', 'mp')
- p_basis: float32 [16384, 128], P('dp')
- q_factor: float32 [28672, 128], P('mp')
The draws below stay inside these ranges and needn't reach their ends.
Inputs may be any that keep to these rules, and one draw needn't show every extreme that they name: `signs`: 1 keeps a row's sign, 0 negates it.
All inputs are finite; a program needn't handle non-finite values.
Results may differ from the reference program's by a relative error of at most 0.0053.
Values may be sent and summed in bfloat16 or wider, within the bound.
No kernel may reach another device: no remote copies, remote signals or barrier semaphores. Data moves between devices by JAX's collectives and lax.ppermute only.
A program may use at most 256 MiB of HBM per device.

```python
import math
import jax
import jax.numpy as jnp
from jax import lax

ROWS = 8192
FF = 28672
RANK = 128
REPLICAS = 2


def place_ends(values, key, smallest, high):
    longest = values.shape.index(max(values.shape))
    spots = []
    for shift in (0, 1):
        where = [jax.random.randint(jax.random.fold_in(key, axis), (), 0, length) for axis, length in enumerate(values.shape)]
        where[longest] = (where[longest] + shift) % values.shape[longest]
        spots.append(tuple(where))
    return values.at[spots[0]].set(smallest).at[spots[1]].set(high)


def steps_of(stream_key, shape, shards, least, high):
    factor_of = 1.0
    for axis_at, shards_of in shards:
        draws = jax.random.uniform(jax.random.fold_in(jax.random.fold_in(stream_key, 6), axis_at), (shards_of,), jnp.float32, least / len(shards), high / len(shards))
        factor_of = factor_of * jnp.repeat(jnp.exp(draws), shape[axis_at] // shards_of).reshape((-1,) + (1,) * (len(shape) - 1 - axis_at))
    return factor_of


def noise(stream_key, dims, deviation, reach, shards=(), kind=jnp.bfloat16):
    result = jax.random.normal(stream_key, dims, jnp.float32) * deviation
    if len(shards) > 0:
        result = steps_of(stream_key, dims, shards, -0.22, 0.18) * result
    return jnp.clip(result, min=-reach, max=reach).astype(kind)


def setup_inputs(seed: int = 0) -> dict:
    splits = jax.random.split(jax.random.key(seed), 4)
    accumulated = noise(splits[0], (REPLICAS * ROWS, FF), 1.0, 6.0, ((0, 4), (1, 8)))
    signs = place_ends(jax.random.randint(splits[1], (ROWS,), 0, 2), jax.random.fold_in(splits[1], 1), 0, 1).astype(jnp.int32)
    q_start = noise(splits[2], (FF, RANK), 1.0, 6.0, ((0, 8),))
    return dict(accumulated=accumulated, signs=signs, q_start=q_start)


def sylvester(size):
    index = jnp.arange(size, dtype=jnp.int32)
    both = index[:, None] & index[None, :]
    parity = jnp.zeros((size, size), jnp.int32)
    for shift in range(max(size.bit_length() - 1, 1)):
        parity = parity ^ both >> shift & 1
    return (1 - 2 * parity).astype(jnp.float32)

def rotate(block):
    total_rows, width = block.shape
    factors = []
    remaining = total_rows
    while remaining > 1:
        factor = min(32, remaining)
        factors.append(factor)
        remaining = remaining // factor
    if len(factors) == 0:
        return block
    cube = block.reshape(tuple(factors) + (width,))
    for which_axis, factor in enumerate(factors):
        cube = jnp.tensordot(sylvester(factor), cube, axes=([1], [which_axis]), precision=lax.Precision.HIGHEST)
        cube = jnp.moveaxis(cube, 0, which_axis)
    return cube.reshape(total_rows, width)

def reference(accumulated, signs, q_start):
    sign = (2 * signs - 1).astype(jnp.float32)
    blocks = accumulated.reshape(REPLICAS, ROWS, FF)

    def rotate_one(block):
        flipped = block.astype(jnp.float32) * sign[:, None]
        return (rotate(flipped) * (1.0 / math.sqrt(ROWS))).astype(jnp.bfloat16)
    rotated = lax.map(rotate_one, blocks)
    rotated = lax.optimization_barrier(rotated)

    def add_projection(total, block):
        return (total + jnp.dot(block.astype(jnp.float32), q_start.astype(jnp.float32), preferred_element_type=jnp.float32), None)
    projected, _ = lax.scan(add_projection, jnp.zeros((ROWS, RANK), jnp.float32), rotated)
    gram = jnp.dot(projected.T, projected, precision=lax.Precision.HIGHEST)
    lower = jnp.linalg.cholesky(gram)
    basis = jax.scipy.linalg.solve_triangular(lower, projected.T, lower=True).T
    basis16 = basis.astype(jnp.bfloat16)

    def add_right(total, block):
        return (total + jnp.dot(block.T.astype(jnp.float32), basis16.astype(jnp.float32), preferred_element_type=jnp.float32), None)
    q_total, _ = lax.scan(add_right, jnp.zeros((FF, RANK), jnp.float32), rotated)
    q_factor = q_total / REPLICAS
    q16 = q_factor.astype(jnp.bfloat16)
    approx = jnp.dot(basis16.astype(jnp.float32), q16.T.astype(jnp.float32), preferred_element_type=jnp.float32)

    def error_one(block):
        return (block.astype(jnp.float32) - approx).astype(jnp.bfloat16)
    new_error = lax.map(error_one, rotated).reshape(REPLICAS * ROWS, FF)
    p_basis = jnp.tile(basis, (REPLICAS, 1))
    return (new_error, p_basis, q_factor)
```

```python
import functools
import math

import jax
import jax.numpy as jnp
from jax import lax
from jax.experimental import pallas as pl
from jax.experimental.pallas import tpu as pltpu
from jax.sharding import Mesh, PartitionSpec as P

REPLICAS = 2
F32 = jnp.float32
BF16 = jnp.bfloat16
VMEM_BYTES = 56 * 1024 * 1024


def sylvester(size):
    index = jnp.arange(size, dtype=jnp.int32)
    parity = lax.population_count(index[:, None] & index[None, :]) & 1
    return (1 - 2 * parity).astype(F32)


def tile_width(columns):
    return 256 if columns % 256 == 0 else 128


def signed_hadamard(signs, position, group, rows):
    side = min(256, rows)
    parts = []
    for distance in range(group):
        other = position ^ distance
        parity = lax.population_count(position & other) & 1
        mine = lax.dynamic_slice_in_dim(signs, other * rows, rows)
        parts.append(((2 * mine - 1) * (1 - 2 * parity)).reshape(rows // side, 1, side))
    table = sylvester(side)[None]
    return jnp.concatenate([table * part.astype(F32) for part in parts], axis=2).astype(BF16)


def rotate_body(group, scale, *refs):
    block_refs, table_ref, out_ref, field_ref = refs[:group], refs[group], refs[group + 1], refs[group + 2]
    count, side, width = field_ref.shape

    @pl.loop(0, count, unroll=4)
    def _(b):
        rows = pl.ds(pl.multiple_of(b * side, side), side)
        stacked = jnp.concatenate([ref[rows, :] for ref in block_refs], axis=0)
        field_ref[b] = jnp.dot(table_ref[b], stacked, preferred_element_type=F32)

    @pl.loop(0, side // 16)
    def _(i):
        inner = pl.multiple_of(i * 16, 16)
        for start in range(0, width, 128):
            lanes = slice(start, start + 128)
            values = [field_ref[b, pl.ds(inner, 16), lanes] for b in range(count)]
            step = 1
            while step < count:
                for b in range(count):
                    if not b & step:
                        low, high = values[b], values[b | step]
                        values[b], values[b | step] = low + high, low - high
                step *= 2
            for b in range(count):
                out_ref[pl.ds(b * side + inner, 16), lanes] = (values[b] * scale).astype(out_ref.dtype)


def rotate(blocks, table, out_type):
    group = len(blocks)
    rows, columns = blocks[0].shape
    count, side, _ = table.shape
    width = tile_width(columns)
    scale = 1.0 / math.sqrt(rows * group)
    strip = pl.BlockSpec((rows, width), lambda j: (0, j))
    return pl.pallas_call(
        functools.partial(rotate_body, group, scale),
        grid=(columns // width,),
        out_shape=jax.ShapeDtypeStruct((rows, columns), out_type),
        in_specs=[strip] * group + [pl.BlockSpec(table.shape, lambda j: (0, 0, 0))],
        out_specs=strip,
        scratch_shapes=[pltpu.VMEM((count, side, width), F32)],
        compiler_params=pltpu.CompilerParams(vmem_limit_bytes=VMEM_BYTES),
        cost_estimate=pl.CostEstimate(
            flops=2 * rows * columns * side * group,
            bytes_accessed=rows * columns * 2 * (group + 1) + table.size * 2,
            transcendentals=0,
        ),
    )(*blocks, table)


def right_body(group, position_ref, *refs):
    del position_ref
    block_refs, left_ref, out_ref = refs[:group], refs[group], refs[group + 1]
    total = jnp.dot(left_ref[0], block_refs[0][...], preferred_element_type=F32)
    for d in range(1, group):
        total += jnp.dot(left_ref[d], block_refs[d][...], preferred_element_type=F32)
    out_ref[...] = total


def right_share(blocks, left, position, share):
    group = len(blocks)
    rows, _ = blocks[0].shape
    rank = left.shape[1]
    width = tile_width(share)
    steps = share // width
    strip = pl.BlockSpec((rows, width), lambda j, where: (0, where[0] * steps + j))
    return pl.pallas_call(
        functools.partial(right_body, group),
        out_shape=jax.ShapeDtypeStruct((rank, share), F32),
        grid_spec=pltpu.PrefetchScalarGridSpec(
            num_scalar_prefetch=1,
            grid=(steps,),
            in_specs=[strip] * group + [pl.BlockSpec(left.shape, lambda j, where: (0, 0, 0))],
            out_specs=pl.BlockSpec((rank, width), lambda j, where: (0, j)),
        ),
        compiler_params=pltpu.CompilerParams(vmem_limit_bytes=VMEM_BYTES),
        cost_estimate=pl.CostEstimate(
            flops=2 * rows * group * share * rank,
            bytes_accessed=rows * share * 2 * group + left.size * 2 + rank * share * 4,
            transcendentals=0,
        ),
    )(position.reshape(1), *blocks, left)


def residual_body(rotated_ref, basis_ref, right_ref, out_ref):
    rows, _ = rotated_ref.shape
    chunk = min(256, rows)

    @pl.loop(0, rows // chunk, unroll=2)
    def _(i):
        part = pl.ds(pl.multiple_of(i * chunk, chunk), chunk)
        approx = jnp.dot(basis_ref[part, :], right_ref[...], preferred_element_type=F32)
        out_ref[part, :] = (rotated_ref[part, :].astype(F32) - approx).astype(out_ref.dtype)


def residual(rotated, basis16, right16):
    rows, columns = rotated.shape
    rank = basis16.shape[1]
    width = tile_width(columns)
    strip = pl.BlockSpec((rows, width), lambda j: (0, j))
    return pl.pallas_call(
        residual_body,
        grid=(columns // width,),
        out_shape=jax.ShapeDtypeStruct((rows, columns), BF16),
        in_specs=[
            strip,
            pl.BlockSpec((rows, rank), lambda j: (0, 0)),
            pl.BlockSpec((rank, width), lambda j: (0, j)),
        ],
        out_specs=strip,
        compiler_params=pltpu.CompilerParams(vmem_limit_bytes=VMEM_BYTES),
        cost_estimate=pl.CostEstimate(
            flops=2 * rows * columns * rank, bytes_accessed=rows * columns * 4, transcendentals=0
        ),
    )(rotated, basis16, right16)


def from_distance(block, axis, distance):
    count = lax.axis_size(axis)
    return lax.ppermute(block, axis, [(p, p ^ distance) for p in range(count)])


def gather_positions(block, position, dimension):
    group = lax.axis_size("pos")
    if group == 2:
        other = from_distance(block, "pos", 1)
        first = position == 0
        return jnp.concatenate(
            [jnp.where(first, block, other), jnp.where(first, other, block)], axis=dimension
        )
    return lax.all_gather(block, "pos", axis=dimension, tiled=True)


def local(accumulated, signs, q_start):
    rows, columns = accumulated.shape
    rank = q_start.shape[1]
    group = lax.axis_size("pos")
    position = lax.axis_index("pos")

    blocks = [accumulated] + [from_distance(accumulated, "pos", d) for d in range(1, group)]
    table = signed_hadamard(signs, position, group, rows)

    partial = jnp.dot(accumulated, q_start, preferred_element_type=F32)
    mine = lax.psum_scatter(partial, ("rep", "mp"), scatter_dimension=0, tiled=True)
    own16 = lax.all_gather(mine.astype(BF16), ("rep", "mp"), axis=0, tiled=True)
    around16 = [own16] + [from_distance(own16, "pos", d) for d in range(1, group)]

    rotated = rotate(blocks, table, BF16)

    everywhere = jnp.stack(around16)
    if group > 2:
        everywhere = lax.all_gather(own16, "pos", axis=0, tiled=False)
    gram = jnp.einsum("grk,grl->kl", everywhere, everywhere, preferred_element_type=F32)
    lower = jnp.linalg.cholesky(gram)
    inverse = jax.scipy.linalg.solve_triangular(lower, jnp.eye(rank, dtype=F32), lower=True)

    share = columns // group
    if share % 128 == 0:
        left = jnp.stack([part.T for part in around16])
        half = right_share(blocks, left, position, share).astype(BF16)
        half = half.astype(F32) + from_distance(half, "rep", 1).astype(F32)
        right_half = jnp.dot(inverse, half, precision=lax.Precision.HIGHEST) / REPLICAS
        right = gather_positions(right_half, position, 1)
    else:
        whole = right_share(blocks[:1], own16.T[None], jnp.zeros((), jnp.int32), columns)
        whole = lax.psum(whole, ("rep", "pos"))
        right = jnp.dot(inverse, whole, precision=lax.Precision.HIGHEST) / REPLICAS

    turned = rotate(around16, table, F32)
    p_basis = jnp.dot(turned, inverse.T, precision=lax.Precision.HIGHEST)
    new_error = residual(rotated, p_basis.astype(BF16), right.astype(BF16))
    return (new_error, p_basis, right.T)


def solution(mesh):
    dp_count, mp_count = mesh.shape["dp"], mesh.shape["mp"]
    fine = Mesh(
        mesh.devices.reshape(REPLICAS, dp_count // REPLICAS, mp_count), ("rep", "pos", "mp")
    )
    rows_of = ("rep", "pos")
    in_specs = (P(rows_of, "mp"), P(), P("mp", None))
    out_specs = (P(rows_of, "mp"), P(rows_of, None), P("mp", None))
    return jax.shard_map(local, mesh=fine, in_specs=in_specs, out_specs=out_specs, check_vma=False)
```

```python
import functools
import math

import jax
import jax.numpy as jnp
from jax import lax
from jax.experimental import pallas as pl
from jax.experimental.pallas import tpu as pltpu
from jax.sharding import Mesh, PartitionSpec as P

REPLICAS = 2
F32 = jnp.float32
BF16 = jnp.bfloat16
ANY = pl.BlockSpec(memory_space=pl.ANY)
PARAMS = pltpu.CompilerParams(vmem_limit_bytes=56 * 1024 * 1024)


def cost(flops, size):
    return pl.CostEstimate(flops=flops, bytes_accessed=size, transcendentals=0)


def sylvester(size):
    index = jnp.arange(size, dtype=jnp.int32)
    parity = lax.population_count(index[:, None] & index[None, :]) & 1
    return (1 - 2 * parity).astype(F32)


def butterflies(values):
    values = list(values)
    step = 1
    while step < len(values):
        for low in range(len(values)):
            if not low & step:
                high = low | step
                values[low], values[high] = values[low] + values[high], values[low] - values[high]
        step *= 2
    return values


def tile_width(columns):
    return 256 if columns % 256 == 0 else 128


def minus_one_to(number):
    return 1 - 2 * (lax.population_count(number) & 1)


def signed_hadamard(signs, position, group, rows):
    side = min(256, rows)
    parts = []
    for distance in range(group):
        mine = lax.dynamic_slice_in_dim(signs, (position ^ distance) * rows, rows)
        parts.append((2 * mine - 1) * minus_one_to(position & distance))
    flips = jnp.stack(parts).astype(F32).reshape(group, rows // side, 1, side)
    return (sylvester(side) * flips).astype(BF16)


def rotate_body(group, outs, *refs):
    scale_ref, table_ref = refs[group], refs[group + 1]
    block_refs, out_refs, field_ref = refs[:group], refs[-1 - outs : -1], refs[-1]
    _, count, side, width = field_ref.shape

    @pl.loop(0, count, unroll=8)
    def _(b):
        rows = pl.ds(pl.multiple_of(b * side, side), side)
        parts = [
            jnp.dot(table_ref[d, b], block_refs[d][rows, :], preferred_element_type=F32) for d in range(group)
        ]
        mixed = butterflies(parts) if outs > 1 else [sum(parts[1:], parts[0])]
        for o in range(outs):
            field_ref[o, b] = mixed[o]

    @pl.loop(0, side // 16)
    def _(i):
        inner = pl.multiple_of(i * 16, 16)
        for o in range(outs):
            for start in range(0, width, 128):
                lanes = slice(start, start + 128)
                values = butterflies([field_ref[o, b, pl.ds(inner, 16), lanes] for b in range(count)])
                for b in range(count):
                    turned = (values[b] * scale_ref[o]).astype(out_refs[o].dtype)
                    out_refs[o][pl.ds(b * side + inner, 16), lanes] = turned


def rotate(blocks, table, position, out_type, outs, after=()):
    group = len(blocks)
    rows, columns = blocks[-1].shape
    _, count, side, _ = table.shape
    width = tile_width(columns)
    steps = columns // width
    distances = jnp.arange(group, dtype=jnp.int32)
    scales = (minus_one_to(position) * minus_one_to(position & distances)).astype(F32) / math.sqrt(rows * group)

    def place(block):
        if block.shape[1] == columns:
            return pl.BlockSpec((rows, width), lambda j, where: (0, j))
        return pl.BlockSpec((rows, width), lambda j, where: (0, where[0] * steps + j))

    def body(where_ref, *refs):
        kept = refs[: group + 2] + refs[group + 2 + len(after) :]
        rotate_body(group, outs, *kept)

    return pl.pallas_call(
        body,
        out_shape=[jax.ShapeDtypeStruct((rows, columns), out_type)] * outs,
        grid_spec=pltpu.PrefetchScalarGridSpec(
            num_scalar_prefetch=1,
            grid=(steps,),
            in_specs=[place(block) for block in blocks]
            + [pl.BlockSpec(memory_space=pltpu.SMEM), pl.BlockSpec(table.shape, lambda j, where: (0, 0, 0, 0))]
            + [ANY] * len(after),
            out_specs=[pl.BlockSpec((rows, width), lambda j, where: (0, j))] * outs,
            scratch_shapes=[pltpu.VMEM((outs, count, side, width), F32)],
        ),
        compiler_params=PARAMS,
        cost_estimate=cost(2 * rows * columns * side * group, rows * columns * 2 * (group + outs) + table.size * 2),
    )(position.reshape(1), *blocks, scales, table, *after)


def project(accumulated, q_start, plane, pieces):
    rows, columns = accumulated.shape
    rank = q_start.shape[1]
    piece = rows // pieces
    tall = min(512, piece)
    steps = piece // tall

    def body(where_ref, a_ref, q_ref, *out_refs):
        at = pl.program_id(0)
        product = jnp.dot(a_ref[...], q_ref[...], preferred_element_type=F32)
        for d in range(pieces):

            @pl.when(at // steps == d)
            def _(d=d):
                out_refs[d][...] = product.astype(out_refs[d].dtype)

    def out_place(d):
        return pl.BlockSpec((tall, rank), lambda i, where: (jnp.clip(i - d * steps, 0, steps - 1), 0))

    return pl.pallas_call(
        body,
        out_shape=[jax.ShapeDtypeStruct((piece, rank), F32 if d == 0 else BF16) for d in range(pieces)],
        grid_spec=pltpu.PrefetchScalarGridSpec(
            num_scalar_prefetch=1,
            grid=(pieces * steps,),
            in_specs=[
                pl.BlockSpec((tall, columns), lambda i, where: ((where[0] ^ (i // steps)) * steps + i % steps, 0)),
                pl.BlockSpec((columns, rank), lambda i, where: (0, 0)),
            ],
            out_specs=[out_place(d) for d in range(pieces)],
        ),
        compiler_params=PARAMS,
        cost_estimate=cost(2 * rows * columns * rank, rows * columns * 2),
    )(plane.reshape(1), accumulated, q_start)


def columns_of(accumulated, owner, share, after):
    rows, _ = accumulated.shape
    width = tile_width(share)
    steps = share // width

    def body(where_ref, a_ref, after_ref, out_ref):
        out_ref[...] = a_ref[...]

    return pl.pallas_call(
        body,
        out_shape=jax.ShapeDtypeStruct((rows, share), accumulated.dtype),
        grid_spec=pltpu.PrefetchScalarGridSpec(
            num_scalar_prefetch=1,
            grid=(steps,),
            in_specs=[pl.BlockSpec((rows, width), lambda j, where: (0, where[0] * steps + j)), ANY],
            out_specs=pl.BlockSpec((rows, width), lambda j, where: (0, j)),
        ),
        compiler_params=PARAMS,
        cost_estimate=cost(0, rows * share * 4),
    )(owner.reshape(1), accumulated, after)


def split_sum(own, others, place, pieces):
    rows, rank = own.shape
    piece = rows // pieces

    def body(where_ref, own_ref, *refs):
        other_refs, out_refs = refs[: len(others)], refs[len(others) :]
        for d in range(pieces):
            at = pl.ds(pl.multiple_of((where_ref[0] ^ d) * piece, piece), piece)
            total = own_ref[at, :]
            for ref in other_refs:
                total += ref[at, :].astype(F32)
            out_refs[d][...] = total.astype(out_refs[d].dtype)

    return pl.pallas_call(
        body,
        out_shape=[jax.ShapeDtypeStruct((piece, rank), F32 if d == 0 else BF16) for d in range(pieces)],
        in_specs=[pl.BlockSpec(memory_space=pltpu.SMEM)] + [pl.BlockSpec(memory_space=pltpu.VMEM)] * (1 + len(others)),
        out_specs=[pl.BlockSpec(memory_space=pltpu.VMEM)] * pieces,
        compiler_params=PARAMS,
    )(place.reshape(1), own, *others)


def assemble(parts, place, after=()):
    rows, rank = parts[0].shape
    count = len(parts)

    def body(where_ref, *refs):
        out_ref = refs[-1]
        for d in range(count):
            at = pl.ds(pl.multiple_of((where_ref[0] ^ d) * rows, rows), rows)
            out_ref[at, :] = refs[d][...]

    return pl.pallas_call(
        body,
        out_shape=jax.ShapeDtypeStruct((rows * count, rank), parts[0].dtype),
        in_specs=[pl.BlockSpec(memory_space=pltpu.SMEM)]
        + [pl.BlockSpec(memory_space=pltpu.VMEM)] * count
        + [ANY] * len(after),
        out_specs=pl.BlockSpec(memory_space=pltpu.VMEM),
        compiler_params=PARAMS,
    )(place.reshape(1), *parts, *after)


def right_share(blocks, lefts, position, share):
    group = len(blocks)
    rows, rank = lefts[0].shape
    width = tile_width(share)
    steps = share // width

    def place(block):
        if block.shape[1] == share:
            return pl.BlockSpec((rows, width), lambda j, where: (0, j))
        return pl.BlockSpec((rows, width), lambda j, where: (0, where[0] * steps + j))

    def body(where_ref, *refs):
        block_refs, left_refs, out_ref, flat_ref = refs[:group], refs[group : 2 * group], refs[-2], refs[-1]

        @pl.when(pl.program_id(0) == 0)
        def _():
            for d in range(group):
                flat_ref[d] = left_refs[d][...].T

        total = jnp.dot(flat_ref[0], block_refs[0][...], preferred_element_type=F32)
        for d in range(1, group):
            total += jnp.dot(flat_ref[d], block_refs[d][...], preferred_element_type=F32)
        out_ref[...] = total

    return pl.pallas_call(
        body,
        out_shape=jax.ShapeDtypeStruct((rank, share), F32),
        grid_spec=pltpu.PrefetchScalarGridSpec(
            num_scalar_prefetch=1,
            grid=(steps,),
            in_specs=[place(block) for block in blocks]
            + [pl.BlockSpec((rows, rank), lambda j, where: (0, 0))] * group,
            out_specs=pl.BlockSpec((rank, width), lambda j, where: (0, j)),
            scratch_shapes=[pltpu.VMEM((group, rank, rows), BF16)],
        ),
        compiler_params=PARAMS,
        cost_estimate=cost(2 * rows * group * share * rank, rows * share * 2 * group),
    )(position.reshape(1), *blocks, *lefts)


def residual(rotated, basis16, right16, columns, owner, into=None):
    rows, share = rotated.shape
    rank = basis16.shape[1]
    width = tile_width(share)
    steps = share // width
    chunk = min(512, rows)
    earlier = () if into is None else (into,)

    def body(where_ref, rotated_ref, basis_ref, right_ref, *refs):
        out_ref = refs[-1]
        for start in range(0, rows, chunk):
            part = slice(start, start + chunk)
            approx = jnp.dot(basis_ref[part, :], right_ref[...], preferred_element_type=F32)
            out_ref[part, :] = (rotated_ref[part, :].astype(F32) - approx).astype(out_ref.dtype)

    return pl.pallas_call(
        body,
        out_shape=jax.ShapeDtypeStruct((rows, columns), BF16),
        grid_spec=pltpu.PrefetchScalarGridSpec(
            num_scalar_prefetch=1,
            grid=(steps,),
            in_specs=[
                pl.BlockSpec((rows, width), lambda j, where: (0, j)),
                pl.BlockSpec((rows, rank), lambda j, where: (0, 0)),
                pl.BlockSpec((rank, width), lambda j, where: (0, j)),
            ]
            + [ANY] * len(earlier),
            out_specs=pl.BlockSpec((rows, width), lambda j, where: (0, where[0] * steps + j)),
        ),
        input_output_aliases={4: 0} if earlier else {},
        compiler_params=PARAMS,
        cost_estimate=cost(2 * rows * share * rank, rows * share * 4),
    )(owner.reshape(1), rotated, basis16, right16, *earlier)


def from_distance(block, axis, distance):
    count = lax.axis_size(axis)
    return lax.ppermute(block, axis, [(p, p ^ distance) for p in range(count)])


def from_plane(block, distance):
    count, mp_count = REPLICAS * lax.axis_size("mp"), lax.axis_size("mp")
    change = (distance & 1) | (distance >> 1) * mp_count
    return lax.ppermute(block, ("rep", "mp"), [(p, p ^ change) for p in range(count)])


def from_line(block, distance):
    return from_distance(block, "mp", distance << 1)


def local(accumulated, signs, q_start):
    rows, columns = accumulated.shape
    rank = q_start.shape[1]
    group = lax.axis_size("pos")
    position = lax.axis_index("pos")
    mp_index = lax.axis_index("mp")
    plane = lax.axis_index("rep") * 2 + (mp_index & 1)
    line, lines = mp_index >> 1, lax.axis_size("mp") // 2
    share = columns // group
    shared = share % 128 == 0

    own, *sent = project(accumulated, q_start, plane, 4)
    came = [from_plane(sent[d - 1], d) for d in range(1, 4)]
    if shared:
        blocks = [accumulated] + [
            from_distance(columns_of(accumulated, position ^ d, share, own), "pos", d) for d in range(1, group)
        ]
    else:
        blocks = [accumulated] + [from_distance(accumulated, "pos", d) for d in range(1, group)]
    table = signed_hadamard(signs, position, group, rows)

    own, *sent = split_sum(own, came, line, lines)
    came = [from_line(sent[d - 1], d) for d in range(1, lines)]
    mine16 = sum([part.astype(F32) for part in came], own).astype(BF16)
    near16 = assemble([mine16] + [from_line(mine16, d) for d in range(1, lines)], line)
    far16 = [from_plane(near16, d) for d in range(1, 4)]
    outs = group if shared else 1
    rotated, *away = rotate(blocks, table, position, BF16, outs, after=(near16,))
    rotated = [rotated] + [from_distance(part, "pos", d + 1) for d, part in enumerate(away)]
    own16 = assemble([near16] + far16, plane, after=(rotated[0],))
    around16 = [own16] + [from_distance(own16, "pos", d) for d in range(1, group)]

    if shared:
        half = right_share(blocks, around16, position, share).astype(BF16)
        half = half.astype(F32) + from_distance(half, "rep", 1).astype(F32)
    else:
        half = right_share(blocks[:1], around16[:1], jnp.zeros((), jnp.int32), columns)
        half = lax.psum(half, ("rep", "pos"))

    everywhere = jnp.stack(around16) if group == 2 else lax.all_gather(own16, "pos", axis=0, tiled=False)
    gram = jnp.einsum("grk,grl->kl", everywhere, everywhere, preferred_element_type=F32)
    lower = jnp.linalg.cholesky(gram)
    inverse = jax.scipy.linalg.solve_triangular(lower, jnp.eye(rank, dtype=F32), lower=True)
    (turned,) = rotate(around16, table, position, F32, 1)
    p_basis = jnp.dot(turned, inverse.T, precision=lax.Precision.HIGHEST)
    basis16 = p_basis.astype(BF16)

    right = jnp.dot(inverse, half, precision=lax.Precision.HIGHEST) / REPLICAS
    if not shared:
        new_error = residual(rotated[0], basis16, right.astype(BF16), columns, jnp.zeros((), jnp.int32))
        return (new_error, p_basis, right.T)
    new_error = None
    rights = [right] + [from_distance(right, "pos", d) for d in range(1, group)]
    for d in range(group):
        new_error = residual(rotated[d], basis16, rights[d].astype(BF16), columns, position ^ d, new_error)
    q_factor = jnp.zeros((columns, rank), F32)
    for d in range(group):
        q_factor = lax.dynamic_update_slice_in_dim(q_factor, rights[d].T, (position ^ d) * share, 0)
    return (new_error, p_basis, q_factor)


def solution(mesh):
    dp_count, mp_count = mesh.shape["dp"], mesh.shape["mp"]
    fine = Mesh(
        mesh.devices.reshape(REPLICAS, dp_count // REPLICAS, mp_count), ("rep", "pos", "mp")
    )
    rows_of = ("rep", "pos")
    in_specs = (P(rows_of, "mp"), P(), P("mp", None))
    out_specs = (P(rows_of, "mp"), P(rows_of, None), P("mp", None))
    return jax.shard_map(local, mesh=fine, in_specs=in_specs, out_specs=out_specs, check_vma=False)
```

```python
import functools
import math

import jax
import jax.numpy as jnp
from jax import lax
from jax.experimental import pallas as pl
from jax.experimental.pallas import tpu as pltpu
from jax.sharding import Mesh, PartitionSpec as P

REPLICAS = 2
PLANE = 2 * REPLICAS
F32 = jnp.float32
BF16 = jnp.bfloat16
ANY = pl.BlockSpec(memory_space=pl.ANY)
VMEM = pl.BlockSpec(memory_space=pltpu.VMEM)
SMEM = pl.BlockSpec(memory_space=pltpu.SMEM)
MIB = 1024 * 1024


def cost(flops, size):
    return pl.CostEstimate(flops=flops, bytes_accessed=size, transcendentals=0)


def params(mib):
    return pltpu.CompilerParams(vmem_limit_bytes=mib * MIB)


def sylvester(size):
    index = jnp.arange(size, dtype=jnp.int32)
    parity = lax.population_count(index[:, None] & index[None, :]) & 1
    return (1 - 2 * parity).astype(F32)


def butterflies(values):
    values = list(values)
    step = 1
    while step < len(values):
        for low in range(len(values)):
            if not low & step:
                high = low | step
                values[low], values[high] = values[low] + values[high], values[low] - values[high]
        step *= 2
    return values


def tile_width(columns):
    return 256 if columns % 256 == 0 else 128


def minus_one_to(number):
    return 1 - 2 * (lax.population_count(number) & 1)


def signed_hadamard(signs, position, group, rows):
    side = min(256, rows)
    parts = []
    for distance in range(group):
        mine = lax.dynamic_slice_in_dim(signs, (position ^ distance) * rows, rows)
        parts.append((2 * mine - 1) * minus_one_to(position & distance))
    flips = jnp.stack(parts).astype(F32).reshape(group, rows // side, 1, side)
    return (sylvester(side) * flips).astype(BF16)


def rotate_body(group, outs, pieces, *refs):
    where_ref, refs = refs[0], refs[1:]
    total = sum(pieces)
    block_refs, at = [], 0
    for number in pieces:
        block_refs.append(refs[at : at + number])
        at += number
    scale_ref, table_ref = refs[total], refs[total + 1]
    fields = 2 if pl.num_programs(0) > 1 else 1
    out_refs, field_refs = refs[-fields - outs : -fields], refs[-fields:]
    _, count, side, width = field_refs[0].shape
    cuts = PLANE if max(pieces) > 1 else 1
    each = count // cuts
    strip = side // count

    def mix(e, inside, field_ref):
        b = (where_ref[1] ^ e) * each + inside
        parts = []
        for d in range(group):
            if pieces[d] > 1:
                array, part = divmod(PLANE - 1 - e, PLANE // pieces[d])
                ref, first = block_refs[d][array], (part * each + inside) * side
            else:
                ref, first = block_refs[d][0], b * side
            rows = pl.ds(pl.multiple_of(first, side), side)
            parts.append(jnp.dot(table_ref[d, b], ref[rows, :], preferred_element_type=F32))
        mixed = butterflies(parts) if outs > 1 else [sum(parts[1:], parts[0])]
        for o in range(outs):
            field_ref[o, b] = mixed[o]

    def spread(i, field_ref):
        for part in range(0, strip, 16):
            inner = pl.multiple_of(i * strip + part, 16)
            for o in range(outs):
                for start in range(0, width, 128):
                    lanes = slice(start, start + 128)
                    values = butterflies([field_ref[o, b, pl.ds(inner, 16), lanes] for b in range(count)])
                    for b in range(count):
                        turned = (values[b] * scale_ref[o]).astype(out_refs[o].dtype)
                        out_refs[o][pl.ds(pl.multiple_of(b * side + inner, 16), 16), lanes] = turned

    def sweep(mixed_ref, spread_ref):
        for e in range(cuts):

            @pl.loop(0, each, unroll=2)
            def _(inside, e=e):
                if mixed_ref is not None:
                    mix(e, inside, mixed_ref)
                if spread_ref is not None:
                    spread(e * each + inside, spread_ref)

    if fields == 1:
        sweep(field_refs[0], None)
        sweep(None, field_refs[0])
        return
    odd = pl.program_id(0) % 2 == 1

    @pl.when(jnp.logical_not(odd))
    def _():
        sweep(field_refs[0], field_refs[1])

    @pl.when(odd)
    def _():
        sweep(field_refs[1], field_refs[0])


def rotate(blocks, table, position, plane, out_type, outs, first=0, steps=None, after=()):
    group = len(blocks)
    pieces = [len(block) for block in blocks]
    rows = sum(piece.shape[0] for piece in blocks[0])
    columns = blocks[-1][0].shape[1]
    _, count, side, _ = table.shape
    width = tile_width(columns)
    tiles = columns // width
    steps = tiles if steps is None else steps
    distances = jnp.arange(group, dtype=jnp.int32)
    scales = (minus_one_to(position) * minus_one_to(position & distances)).astype(F32) / math.sqrt(rows * group)
    where = jnp.stack([position, plane if max(pieces) > 1 else jnp.zeros_like(plane)])

    fields = 2 if steps > 1 else 1

    def place(piece):
        def index(j, where):
            j = first + jnp.minimum(j, steps - 1)
            return 0, j if piece.shape[1] == columns else where[0] * tiles + j

        return pl.BlockSpec((piece.shape[0], width), index)

    flat = [piece for block in blocks for piece in block]
    kept = 1 + len(flat) + 2

    def body(*refs):
        rotate_body(group, outs, pieces, *refs[:kept], *refs[kept + len(after) :])

    size = rows * steps * width
    return pl.pallas_call(
        body,
        out_shape=[jax.ShapeDtypeStruct((rows, steps * width), out_type)] * outs,
        grid_spec=pltpu.PrefetchScalarGridSpec(
            num_scalar_prefetch=1,
            grid=(steps + fields - 1,),
            in_specs=[place(piece) for piece in flat]
            + [pl.BlockSpec(memory_space=pltpu.SMEM), pl.BlockSpec(table.shape, lambda j, where: (0, 0, 0, 0))]
            + [ANY] * len(after),
            out_specs=[pl.BlockSpec((rows, width), lambda j, where: (0, jnp.maximum(j - (fields - 1), 0)))] * outs,
            scratch_shapes=[pltpu.VMEM((outs, count, side, width), F32)] * fields,
        ),
        compiler_params=params(24),
        cost_estimate=cost(2 * size * side * group, size * 2 * (group + outs) + table.size * 2),
    )(where, *flat, scales, table, *after)


def scales_of(position, group, rows):
    distances = jnp.arange(group, dtype=jnp.int32)
    return (minus_one_to(position) * minus_one_to(position & distances)).astype(F32) / math.sqrt(rows * group)


def rotate_and_right(blocks, table, lefts, position, plane):
    group = len(blocks)
    pieces = [len(block) for block in blocks]
    rows = blocks[0][0].shape[0]
    rank = lefts[0].shape[1]
    columns = blocks[-1][0].shape[1]
    _, count, side, _ = table.shape
    width = tile_width(columns)
    tiles = columns // width
    each = count // PLANE
    strip = side // count
    where = jnp.stack([position, plane >> 1])

    def body(where_ref, *refs):
        at, block_refs = 0, []
        for number in pieces:
            block_refs.append(refs[at : at + number])
            at += number
        scale_ref, table_ref = refs[at : at + 2]
        left_refs, out_refs = refs[at + 2 : at + 2 + group], refs[at + 2 + group : at + 2 + 2 * group]
        right_ref, even_ref, odd_ref, flat_ref = refs[-4:]
        step = pl.program_id(0)
        shown = jnp.maximum(step - 1, 0) * width

        def block_rows(d, number, first, size):
            if pieces[d] > 1:
                return block_refs[d][1 - number][pl.ds(first, size), :]
            pair = rows // 2
            start = pl.multiple_of((where_ref[1] ^ number) * pair + first, side)
            return block_refs[d][0][pl.ds(start, size), :]

        def mix(number, inside, field_ref):
            b = (where_ref[1] ^ number) * (count // 2) + inside
            first = pl.multiple_of(inside * side, side)
            parts = [
                jnp.dot(table_ref[d, b], block_rows(d, number, first, side), preferred_element_type=F32)
                for d in range(group)
            ]
            for o, mixed in enumerate(butterflies(parts)):
                field_ref[o, b] = mixed

        def spread(i, field_ref):
            for part in range(0, strip, 16):
                inner = pl.multiple_of(i * strip + part, 16)
                for o in range(group):
                    for start in range(0, width, 128):
                        lanes = slice(start, start + 128)
                        values = butterflies([field_ref[o, b, pl.ds(inner, 16), lanes] for b in range(count)])
                        if o == 0:
                            lanes = pl.ds(pl.multiple_of(shown + start, 128), 128)
                        for b in range(count):
                            turned = (values[b] * scale_ref[o]).astype(BF16)
                            out_refs[o][pl.ds(pl.multiple_of(b * side + inner, 16), 16), lanes] = turned

        def sweep(mixed_ref, spread_ref):
            for number in range(2):

                @pl.loop(0, count // 2, unroll=2)
                def _(inside, number=number):
                    mix(number, inside, mixed_ref)
                    spread(number * (count // 2) + inside, spread_ref)

        @pl.when(step == 0)
        def _():
            for d in range(group):
                flat_ref[d] = left_refs[d][...].T

        total = jnp.zeros((rank, width), F32)
        for d in range(group):
            for number in range(2):
                first = pl.multiple_of((where_ref[1] ^ number) * (rows // 2), 128)
                flat = flat_ref[d, :, pl.ds(first, rows // 2)]
                total += jnp.dot(flat, block_rows(d, number, 0, rows // 2), preferred_element_type=F32)
        right_ref[...] = total

        @pl.when(step % 2 == 0)
        def _():
            sweep(even_ref, odd_ref)

        @pl.when(step % 2 == 1)
        def _():
            sweep(odd_ref, even_ref)

    def place(piece):
        def index(j, where):
            j = jnp.minimum(j, tiles - 1)
            return 0, j if piece.shape[1] == columns else where[0] * tiles + j

        return pl.BlockSpec((piece.shape[0], width), index)

    flat = [piece for block in blocks for piece in block]
    field = pltpu.VMEM((group, count, side, width), F32)
    size = rows * columns
    return pl.pallas_call(
        body,
        out_shape=[pltpu.VMEM((rows, columns), BF16)]
        + [jax.ShapeDtypeStruct((rows, columns), BF16)] * (group - 1)
        + [jax.ShapeDtypeStruct((rank, columns), F32)],
        grid_spec=pltpu.PrefetchScalarGridSpec(
            num_scalar_prefetch=1,
            grid=(tiles + 1,),
            in_specs=[place(piece) for piece in flat] + [SMEM, VMEM] + [VMEM] * group,
            out_specs=[VMEM]
            + [pl.BlockSpec((rows, width), lambda j, where: (0, jnp.maximum(j - 1, 0)))] * (group - 1)
            + [pl.BlockSpec((rank, width), lambda j, where: (0, jnp.minimum(j, tiles - 1)))],
            scratch_shapes=[field, field, pltpu.VMEM((group, rank, rows), BF16)],
        ),
        compiler_params=params(38),
        cost_estimate=cost(2 * size * (side + rank) * group, size * 2 * (2 * group - 1) + table.size * 2),
    )(where, *flat, scales_of(position, group, rows), table, *lefts)


def project(accumulated, q_start, piece_at, position, group, pieces, out_type, after, copies):
    rows, columns = accumulated.shape
    rank = q_start.shape[1]
    share = columns // group
    piece = rows // pieces
    tall = min(512, piece)
    steps = piece // tall

    def body(where_ref, a_ref, q_ref, *refs):
        out_refs = refs[len(after) + len(copies) :]
        out_refs[0][...] = jnp.dot(a_ref[...], q_ref[...], preferred_element_type=F32).astype(out_type)
        for d in range(1, group):
            lanes = pl.ds(pl.multiple_of((where_ref[1] ^ d) * share, 128), share)
            out_refs[d][...] = a_ref[:, lanes]

    return pl.pallas_call(
        body,
        out_shape=[jax.ShapeDtypeStruct((piece, rank), out_type)]
        + [jax.ShapeDtypeStruct((2 * piece, share), BF16)] * (group - 1),
        grid_spec=pltpu.PrefetchScalarGridSpec(
            num_scalar_prefetch=1,
            grid=(steps,),
            in_specs=[
                pl.BlockSpec((tall, columns), lambda i, where: (where[0] * steps + i, 0)),
                pl.BlockSpec((columns, rank), lambda i, where: (0, 0)),
            ]
            + [ANY] * (len(after) + len(copies)),
            out_specs=[pl.BlockSpec((tall, rank), lambda i, where: (i, 0))]
            + [pl.BlockSpec((tall, share), lambda i, where: ((where[0] & 1) * steps + i, 0))] * (group - 1),
        ),
        input_output_aliases={3 + len(after) + d: 1 + d for d in range(len(copies))},
        compiler_params=params(24),
        cost_estimate=cost(2 * piece * columns * rank, piece * columns * 3),
    )(jnp.stack([piece_at, position]), accumulated, q_start, *after, *copies)


def split_sum(own, others, place, pieces):
    rows, rank = own.shape
    piece = rows // pieces

    def body(where_ref, own_ref, *refs):
        other_refs, out_refs = refs[: len(others)], refs[len(others) :]
        for d in range(pieces):
            at = pl.ds(pl.multiple_of((where_ref[0] ^ d) * piece, piece), piece)
            total = own_ref[at, :]
            for ref in other_refs:
                total += ref[at, :].astype(F32)
            out_refs[d][...] = total.astype(out_refs[d].dtype)

    return pl.pallas_call(
        body,
        out_shape=[jax.ShapeDtypeStruct((piece, rank), F32 if d == 0 else BF16) for d in range(pieces)],
        in_specs=[pl.BlockSpec(memory_space=pltpu.SMEM)] + [pl.BlockSpec(memory_space=pltpu.VMEM)] * (1 + len(others)),
        out_specs=[pl.BlockSpec(memory_space=pltpu.VMEM)] * pieces,
        compiler_params=params(24),
    )(place.reshape(1), own, *others)


def assemble(parts, place, after=()):
    rows, rank = parts[0].shape
    count = len(parts)

    def body(where_ref, *refs):
        out_ref = refs[-1]
        for d in range(count):
            at = pl.ds(pl.multiple_of((where_ref[0] ^ d) * rows, rows), rows)
            out_ref[at, :] = refs[d][...]

    return pl.pallas_call(
        body,
        out_shape=jax.ShapeDtypeStruct((rows * count, rank), parts[0].dtype),
        in_specs=[pl.BlockSpec(memory_space=pltpu.SMEM)]
        + [pl.BlockSpec(memory_space=pltpu.VMEM)] * count
        + [ANY] * len(after),
        out_specs=pl.BlockSpec(memory_space=pltpu.VMEM),
        compiler_params=params(24),
    )(place.reshape(1), *parts, *after)


def right_piece(accumulated, left, piece_at, position, shares, earlier):
    rows, columns = accumulated.shape
    piece, rank = left.shape
    share = columns // shares
    width = 896 if share % 896 == 0 else tile_width(share)
    steps = columns // width
    each = steps // shares

    def body(where_ref, a_ref, left_ref, *refs):
        out_refs, gram_ref, turned_ref = refs[len(earlier) : -2], refs[-2], refs[-1]
        at = pl.program_id(0)

        @pl.when(at == 0)
        def _():
            turned_ref[...] = left_ref[...].T
            gram_ref[...] = jnp.dot(turned_ref[...], left_ref[...], preferred_element_type=F32)

        total = jnp.dot(turned_ref[...], a_ref[...], preferred_element_type=F32)
        if earlier:
            total += refs[0][...]
        for d in range(shares):

            @pl.when(at // each == where_ref[1] ^ d)
            def _(d=d):
                out_refs[d][...] = total

    def out_place(d):
        return pl.BlockSpec((rank, width), lambda j, where: (0, jnp.clip(j - (where[1] ^ d) * each, 0, each - 1)))

    whole = pl.BlockSpec((rank, width), lambda j, where: (0, j))
    return pl.pallas_call(
        body,
        out_shape=[jax.ShapeDtypeStruct((rank, share), F32)] * shares + [jax.ShapeDtypeStruct((rank, rank), F32)],
        grid_spec=pltpu.PrefetchScalarGridSpec(
            num_scalar_prefetch=1,
            grid=(steps,),
            in_specs=[
                pl.BlockSpec((piece, width), lambda j, where: (where[0], j)),
                pl.BlockSpec((piece, rank), lambda j, where: (0, 0)),
            ]
            + [whole] * len(earlier),
            out_specs=([out_place(d) for d in range(shares)] if shares > 1 else [whole])
            + [pl.BlockSpec((rank, rank), lambda j, where: (0, 0))],
            scratch_shapes=[pltpu.VMEM((rank, piece), BF16)],
        ),
        compiler_params=params(24),
        cost_estimate=cost(2 * piece * columns * rank, piece * columns * 2),
    )(jnp.stack([piece_at, position if shares > 1 else jnp.zeros_like(position)]), accumulated, left, *earlier)


def halves(value):
    high = value.astype(BF16)
    return high, (value - high.astype(F32)).astype(BF16)


def inverse_factor(gram):
    rank = gram.shape[0]
    lane = lax.broadcasted_iota(jnp.int32, (8, rank), 1)
    row = lax.broadcasted_iota(jnp.int32, (8, rank), 0)
    left = [gram[start : start + 8, :] for start in range(0, rank, 8)]
    right = [jnp.where(lane == row + start, 1.0, 0.0).astype(F32) for start in range(0, rank, 8)]
    scales = [jnp.zeros((8, rank), F32)] * len(left)
    for k in range(rank):
        home, inside = divmod(k, 8)
        pivot_row = left[home][inside : inside + 1, :]
        pivot = left[home][inside : inside + 1, k : k + 1]
        made_row = right[home][inside : inside + 1, :]
        inverse = 1.0 / pivot
        scales[home] = jnp.where(row == inside, lax.rsqrt(jnp.broadcast_to(pivot, (8, rank))), scales[home])
        pivot_row, made_row = pivot_row * inverse, made_row * inverse
        for block in range(home, len(left)):
            if block == home and inside == 7:
                continue
            factor = jnp.broadcast_to(left[block][:, k : k + 1], (8, rank))
            if block == home:
                factor = jnp.where(row > inside, factor, 0.0)
            left[block] = left[block] - factor * pivot_row
            right[block] = right[block] - factor * made_row
    return jnp.concatenate([part * scale for part, scale in zip(right, scales)], axis=0)


def basis_of(blocks, table, position):
    group = len(blocks)
    rows, rank = blocks[0].shape
    _, count, side, _ = table.shape

    def body(*refs):
        block_refs, scale_ref, table_ref = refs[:group], refs[group], refs[group + 1]
        inverse_ref, basis_ref, basis16_ref, field_ref, turned_ref = refs[group + 2 :]

        @pl.loop(0, count, unroll=4)
        def _(b):
            at = pl.ds(pl.multiple_of(b * side, side), side)
            mixed = jnp.dot(table_ref[0, b], block_refs[0][at, :], preferred_element_type=F32)
            for d in range(1, group):
                mixed += jnp.dot(table_ref[d, b], block_refs[d][at, :], preferred_element_type=F32)
            field_ref[b] = mixed

        @pl.loop(0, side // 16, unroll=2)
        def _(i):
            inner = pl.multiple_of(i * 16, 16)
            values = butterflies([field_ref[b, pl.ds(inner, 16), :] for b in range(count)])
            for b in range(count):
                turned_ref[pl.ds(pl.multiple_of(b * side + inner, 16), 16), :] = values[b] * scale_ref[0]

        grams = [jnp.dot(ref[...].T, ref[...], preferred_element_type=F32) for ref in block_refs]
        while len(grams) > 1:
            grams = [low + high for low, high in zip(grams[::2], grams[1::2])]
        inverse = inverse_factor(grams[0])
        inverse_ref[...] = inverse
        high, low = halves(inverse.T)
        turned_high, turned_low = halves(turned_ref[...])
        both = jnp.concatenate([turned_high, turned_low], axis=1)
        basis = jnp.dot(both, jnp.concatenate([high, high], axis=0), preferred_element_type=F32)
        basis += jnp.dot(turned_high, low, preferred_element_type=F32)
        basis_ref[...] = basis
        basis16_ref[...] = basis.astype(BF16)

    return pl.pallas_call(
        body,
        out_shape=[
            jax.ShapeDtypeStruct((rank, rank), F32),
            jax.ShapeDtypeStruct((rows, rank), F32),
            jax.ShapeDtypeStruct((rows, rank), BF16),
        ],
        in_specs=[VMEM] * group + [SMEM, VMEM],
        out_specs=[VMEM] * 3,
        scratch_shapes=[pltpu.VMEM((count, side, rank), F32), pltpu.VMEM((rows, rank), F32)],
        compiler_params=params(28),
        cost_estimate=cost(8 * 10**9, 60 * 10**6),
    )(*blocks, scales_of(position, group, rows), table)


def residual(rotated, basis16, right16, columns, owner, into=None, resident=False):
    rows, share = rotated.shape
    rank = right16.shape[0]
    tall = min(512, rows)
    earlier = () if into is None else (into,)

    def body(where_ref, rotated_ref, basis_ref, right_ref, *refs):
        out_ref = refs[-1]
        part = slice(None)
        if resident:
            part = pl.ds(pl.multiple_of(pl.program_id(0) * tall, tall), tall)
        for start in range(0, share, 256):
            lanes = slice(start, min(start + 256, share))
            approx = jnp.dot(basis_ref[...], right_ref[:, lanes], preferred_element_type=F32)
            out_ref[:, lanes] = (rotated_ref[part, lanes].astype(F32) - approx).astype(out_ref.dtype)

    return pl.pallas_call(
        body,
        out_shape=jax.ShapeDtypeStruct((rows, columns), BF16),
        grid_spec=pltpu.PrefetchScalarGridSpec(
            num_scalar_prefetch=1,
            grid=(rows // tall,),
            in_specs=[
                VMEM if resident else pl.BlockSpec((tall, share), lambda i, where: (i, 0)),
                pl.BlockSpec((tall, rank), lambda i, where: (i, 0)),
                pl.BlockSpec((rank, share), lambda i, where: (0, 0)),
            ]
            + [ANY] * len(earlier),
            out_specs=pl.BlockSpec((tall, share), lambda i, where: (i, where[0])),
        ),
        input_output_aliases={4: 0} if earlier else {},
        compiler_params=params(32 if resident else 16),
        cost_estimate=cost(2 * rows * share * rank, rows * share * 4),
    )(owner.reshape(1), rotated, basis16, right16, *earlier)


def from_distance(block, axis, distance):
    count = lax.axis_size(axis)
    return lax.ppermute(block, axis, [(p, p ^ distance) for p in range(count)])


def from_plane(block, distance):
    count, mp_count = REPLICAS * lax.axis_size("mp"), lax.axis_size("mp")
    change = (distance & 1) | (distance >> 1) * mp_count
    return lax.ppermute(block, ("rep", "mp"), [(p, p ^ change) for p in range(count)])


def from_line(block, distance):
    return from_distance(block, "mp", distance << 1)


def local(accumulated, signs, q_start):
    rows, columns = accumulated.shape
    rank = q_start.shape[1]
    group = lax.axis_size("pos")
    position = lax.axis_index("pos")
    mp_index = lax.axis_index("mp")
    plane = lax.axis_index("rep") * 2 + (mp_index & 1)
    line, lines = mp_index >> 1, lax.axis_size("mp") // 2
    share = columns // group
    shared = share % 128 == 0 and rows % (256 * PLANE) == 0
    others = range(1, group)

    came, after, copies = [], (), []
    other_pieces = [[] for _ in others]
    for d in reversed(range(PLANE)):
        out_type = BF16 if d else F32
        part, *copies = project(
            accumulated, q_start, plane ^ d, position, group if shared else 1, PLANE, out_type, after, copies
        )
        after = (part,)
        if d:
            came.append(from_plane(part, d))
        if d == 1:
            after = (part, came[0])
        if d % 2 == 0:
            for e, copy in enumerate(copies):
                other_pieces[e].append(from_distance(copy, "pos", e + 1))
            copies = []
    table = signed_hadamard(signs, position, group, rows)
    if not shared:
        other_pieces = [[from_distance(accumulated, "pos", d)] for d in others]
    blocks = [[accumulated]] + other_pieces

    own, *sent = split_sum(part, came, line, lines)
    came = [from_line(sent[d - 1], d) for d in range(1, lines)]
    mine16 = sum([part.astype(F32) for part in came], own).astype(BF16)
    near16 = assemble([mine16] + [from_line(mine16, d) for d in range(1, lines)], line)
    far16 = [near16] + [from_plane(near16, d) for d in range(1, PLANE)]
    own16 = assemble(far16, plane)
    around16 = [own16] + [from_distance(own16, "pos", d) for d in others]

    if shared:
        *rotated, half = rotate_and_right(blocks, table, around16, position, plane)
        half = half.astype(BF16)
        rotated = rotated[:1] + [from_distance(part, "pos", d + 1) for d, part in enumerate(rotated[1:])]
        half = half.astype(F32) + from_distance(half, "rep", 1).astype(F32)
    else:
        rotated = rotate(blocks, table, position, plane, BF16, 1)
        totals = []
        for d in range(PLANE):
            *totals, _ = right_piece(accumulated, far16[d], plane ^ d, position, 1, totals)
        half = lax.psum(totals[0], ("rep", "pos"))
    inverse, p_basis, basis16 = basis_of(around16, table, position)

    right = jnp.dot(inverse, half, precision=lax.Precision.HIGHEST) / REPLICAS
    if not shared:
        new_error = residual(rotated[0], basis16, right.astype(BF16), columns, jnp.zeros((), jnp.int32))
        return (new_error, p_basis, right.T)
    new_error = None
    rights = [right] + [from_distance(right, "pos", d) for d in others]
    for d in range(group):
        new_error = residual(
            rotated[d], basis16, rights[d].astype(BF16), columns, position ^ d, new_error, d == 0
        )
    q_factor = jnp.zeros((columns, rank), F32)
    for d in range(group):
        q_factor = lax.dynamic_update_slice_in_dim(q_factor, rights[d].T, (position ^ d) * share, 0)
    return (new_error, p_basis, q_factor)


def solution(mesh):
    dp_count, mp_count = mesh.shape["dp"], mesh.shape["mp"]
    fine = Mesh(
        mesh.devices.reshape(REPLICAS, dp_count // REPLICAS, mp_count), ("rep", "pos", "mp")
    )
    rows_of = ("rep", "pos")
    in_specs = (P(rows_of, "mp"), P(), P("mp", None))
    out_specs = (P(rows_of, "mp"), P(rows_of, None), P("mp", None))
    return jax.shard_map(local, mesh=fine, in_specs=in_specs, out_specs=out_specs, check_vma=False)
```

```python
import functools
import math

import jax
import jax.numpy as jnp
from jax import lax
from jax.experimental import pallas as pl
from jax.experimental.pallas import tpu as pltpu
from jax.sharding import Mesh, PartitionSpec as P

REPLICAS = 2
PLANE = 2 * REPLICAS
F32 = jnp.float32
BF16 = jnp.bfloat16
ANY = pl.BlockSpec(memory_space=pl.ANY)
VMEM = pl.BlockSpec(memory_space=pltpu.VMEM)
SMEM = pl.BlockSpec(memory_space=pltpu.SMEM)
MIB = 1024 * 1024


def cost(flops, size):
    return pl.CostEstimate(flops=flops, bytes_accessed=size, transcendentals=0)


def params(mib):
    return pltpu.CompilerParams(vmem_limit_bytes=mib * MIB)


def sylvester(size):
    index = jnp.arange(size, dtype=jnp.int32)
    parity = lax.population_count(index[:, None] & index[None, :]) & 1
    return (1 - 2 * parity).astype(F32)


def butterflies(values):
    values = list(values)
    step = 1
    while step < len(values):
        for low in range(len(values)):
            if not low & step:
                high = low | step
                values[low], values[high] = values[low] + values[high], values[low] - values[high]
        step *= 2
    return values


def tile_width(columns):
    return 256 if columns % 256 == 0 else 128


def minus_one_to(number):
    return 1 - 2 * (lax.population_count(number) & 1)


def signed_hadamard(signs, position, group, rows):
    side = min(256, rows)
    parts = []
    for distance in range(group):
        mine = lax.dynamic_slice_in_dim(signs, (position ^ distance) * rows, rows)
        parts.append((2 * mine - 1) * minus_one_to(position & distance))
    flips = jnp.stack(parts).astype(F32).reshape(group, rows // side, 1, side)
    return (sylvester(side) * flips).astype(BF16)


def rotate_body(group, outs, pieces, *refs):
    where_ref, refs = refs[0], refs[1:]
    total = sum(pieces)
    block_refs, at = [], 0
    for number in pieces:
        block_refs.append(refs[at : at + number])
        at += number
    scale_ref, table_ref = refs[total], refs[total + 1]
    fields = 2 if pl.num_programs(0) > 1 else 1
    out_refs, field_refs = refs[-fields - outs : -fields], refs[-fields:]
    _, count, side, width = field_refs[0].shape
    cuts = PLANE if max(pieces) > 1 else 1
    each = count // cuts
    strip = side // count

    def mix(e, inside, field_ref):
        b = (where_ref[1] ^ e) * each + inside
        parts = []
        for d in range(group):
            if pieces[d] > 1:
                array, part = divmod(PLANE - 1 - e, PLANE // pieces[d])
                ref, first = block_refs[d][array], (part * each + inside) * side
            else:
                ref, first = block_refs[d][0], b * side
            rows = pl.ds(pl.multiple_of(first, side), side)
            parts.append(jnp.dot(table_ref[d, b], ref[rows, :], preferred_element_type=F32))
        mixed = butterflies(parts) if outs > 1 else [sum(parts[1:], parts[0])]
        for o in range(outs):
            field_ref[o, b] = mixed[o]

    def spread(i, field_ref):
        for part in range(0, strip, 16):
            inner = pl.multiple_of(i * strip + part, 16)
            for o in range(outs):
                for start in range(0, width, 128):
                    lanes = slice(start, start + 128)
                    values = butterflies([field_ref[o, b, pl.ds(inner, 16), lanes] for b in range(count)])
                    for b in range(count):
                        turned = (values[b] * scale_ref[o]).astype(out_refs[o].dtype)
                        out_refs[o][pl.ds(pl.multiple_of(b * side + inner, 16), 16), lanes] = turned

    def sweep(mixed_ref, spread_ref):
        for e in range(cuts):

            @pl.loop(0, each, unroll=2)
            def _(inside, e=e):
                if mixed_ref is not None:
                    mix(e, inside, mixed_ref)
                if spread_ref is not None:
                    spread(e * each + inside, spread_ref)

    if fields == 1:
        sweep(field_refs[0], None)
        sweep(None, field_refs[0])
        return
    odd = pl.program_id(0) % 2 == 1

    @pl.when(jnp.logical_not(odd))
    def _():
        sweep(field_refs[0], field_refs[1])

    @pl.when(odd)
    def _():
        sweep(field_refs[1], field_refs[0])


def rotate(blocks, table, position, plane, out_type, outs, first=0, steps=None, after=()):
    group = len(blocks)
    pieces = [len(block) for block in blocks]
    rows = sum(piece.shape[0] for piece in blocks[0])
    columns = blocks[-1][0].shape[1]
    _, count, side, _ = table.shape
    width = tile_width(columns)
    tiles = columns // width
    steps = tiles if steps is None else steps
    distances = jnp.arange(group, dtype=jnp.int32)
    scales = (minus_one_to(position) * minus_one_to(position & distances)).astype(F32) / math.sqrt(rows * group)
    where = jnp.stack([position, plane if max(pieces) > 1 else jnp.zeros_like(plane)])

    fields = 2 if steps > 1 else 1

    def place(piece):
        def index(j, where):
            j = first + jnp.minimum(j, steps - 1)
            return 0, j if piece.shape[1] == columns else where[0] * tiles + j

        return pl.BlockSpec((piece.shape[0], width), index)

    flat = [piece for block in blocks for piece in block]
    kept = 1 + len(flat) + 2

    def body(*refs):
        rotate_body(group, outs, pieces, *refs[:kept], *refs[kept + len(after) :])

    size = rows * steps * width
    return pl.pallas_call(
        body,
        out_shape=[jax.ShapeDtypeStruct((rows, steps * width), out_type)] * outs,
        grid_spec=pltpu.PrefetchScalarGridSpec(
            num_scalar_prefetch=1,
            grid=(steps + fields - 1,),
            in_specs=[place(piece) for piece in flat]
            + [pl.BlockSpec(memory_space=pltpu.SMEM), pl.BlockSpec(table.shape, lambda j, where: (0, 0, 0, 0))]
            + [ANY] * len(after),
            out_specs=[pl.BlockSpec((rows, width), lambda j, where: (0, jnp.maximum(j - (fields - 1), 0)))] * outs,
            scratch_shapes=[pltpu.VMEM((outs, count, side, width), F32)] * fields,
        ),
        compiler_params=params(24),
        cost_estimate=cost(2 * size * side * group, size * 2 * (group + outs) + table.size * 2),
    )(where, *flat, scales, table, *after)


def scales_of(position, group, rows):
    distances = jnp.arange(group, dtype=jnp.int32)
    return (minus_one_to(position) * minus_one_to(position & distances)).astype(F32) / math.sqrt(rows * group)


def rotate_and_right(blocks, table, lefts, position, plane):
    group = len(blocks)
    pieces = [len(block) for block in blocks]
    rows = blocks[0][0].shape[0]
    rank = lefts[0].shape[1]
    columns = blocks[-1][0].shape[1]
    _, count, side, _ = table.shape
    width = tile_width(columns)
    tiles = columns // width
    each = count // PLANE
    strip = side // count
    where = jnp.stack([position, plane >> 1])

    def body(where_ref, *refs):
        at, block_refs = 0, []
        for number in pieces:
            block_refs.append(refs[at : at + number])
            at += number
        scale_ref, table_ref = refs[at : at + 2]
        left_refs, out_refs = refs[at + 2 : at + 2 + group], refs[at + 2 + group : at + 2 + 2 * group]
        right_ref, even_ref, odd_ref, both_ref = refs[-4:]
        step = pl.program_id(0)
        shown = jnp.maximum(step - 1, 0) * width

        def block_rows(d, number, first, size):
            if pieces[d] > 1:
                return block_refs[d][1 - number][pl.ds(first, size), :]
            pair = rows // 2
            start = pl.multiple_of((where_ref[1] ^ number) * pair + first, side)
            return block_refs[d][0][pl.ds(start, size), :]

        def mix(number, inside, field_ref):
            b = (where_ref[1] ^ number) * (count // 2) + inside
            first = pl.multiple_of(inside * side, side)
            products = [
                jnp.dot(both_ref[d, b], block_rows(d, number, first, side), preferred_element_type=F32)
                for d in range(group)
            ]
            right_ref[...] += sum([product[side:] for product in products[1:]], products[0][side:])
            for o, mixed in enumerate(butterflies([product[:side] for product in products])):
                field_ref[o, b] = mixed

        def spread(i, field_ref):
            for part in range(0, strip, 16):
                inner = pl.multiple_of(i * strip + part, 16)
                for o in range(group):
                    for start in range(0, width, 128):
                        lanes = slice(start, start + 128)
                        values = butterflies([field_ref[o, b, pl.ds(inner, 16), lanes] for b in range(count)])
                        if o == 0:
                            lanes = pl.ds(pl.multiple_of(shown + start, 128), 128)
                        for b in range(count):
                            turned = (values[b] * scale_ref[o]).astype(BF16)
                            out_refs[o][pl.ds(pl.multiple_of(b * side + inner, 16), 16), lanes] = turned

        def sweep(mixed_ref, spread_ref):
            for number in range(2):

                @pl.loop(0, count // 2, unroll=2)
                def _(inside, number=number):
                    if mixed_ref is not None:
                        mix(number, inside, mixed_ref)
                    if spread_ref is not None:
                        spread(number * (count // 2) + inside, spread_ref)

        @pl.when(step == 0)
        def _():
            for d in range(group):
                for b in range(count):
                    both_ref[d, b, :side, :] = table_ref[d, b]
                    both_ref[d, b, side:, :] = left_refs[d][b * side : (b + 1) * side, :].T

        @pl.when(step < tiles)
        def _():
            right_ref[...] = jnp.zeros_like(right_ref)

        fields = (even_ref, odd_ref)

        @pl.when(step == 0)
        def _():
            sweep(fields[0], None)

        for parity in range(2):

            @pl.when((step > 0) & (step < tiles) & (step % 2 == parity))
            def _(parity=parity):
                sweep(fields[parity], fields[1 - parity])

        @pl.when(step == tiles)
        def _():
            sweep(None, fields[(tiles - 1) % 2])

    def place(piece):
        def index(j, where):
            j = jnp.minimum(j, tiles - 1)
            return 0, j if piece.shape[1] == columns else where[0] * tiles + j

        return pl.BlockSpec((piece.shape[0], width), index)

    flat = [piece for block in blocks for piece in block]
    field = pltpu.VMEM((group, count, side, width), F32)
    size = rows * columns
    return pl.pallas_call(
        body,
        out_shape=[pltpu.VMEM((rows, columns), BF16)]
        + [jax.ShapeDtypeStruct((rows, columns), BF16)] * (group - 1)
        + [jax.ShapeDtypeStruct((rank, columns), F32)],
        grid_spec=pltpu.PrefetchScalarGridSpec(
            num_scalar_prefetch=1,
            grid=(tiles + 1,),
            in_specs=[place(piece) for piece in flat] + [SMEM, VMEM] + [VMEM] * group,
            out_specs=[VMEM]
            + [pl.BlockSpec((rows, width), lambda j, where: (0, jnp.maximum(j - 1, 0)))] * (group - 1)
            + [pl.BlockSpec((rank, width), lambda j, where: (0, jnp.minimum(j, tiles - 1)))],
            scratch_shapes=[field, field, pltpu.VMEM((group, count, side + rank, side), BF16)],
        ),
        compiler_params=params(41),
        cost_estimate=cost(2 * size * (side + rank) * group, size * 2 * (2 * group - 1) + table.size * 2),
    )(where, *flat, scales_of(position, group, rows), table, *lefts)


def project(accumulated, q_start, piece_at, position, group, out_types, after):
    rows, columns = accumulated.shape
    rank = q_start.shape[1]
    share = columns // group
    piece = rows // PLANE
    tall = min(512, piece)
    steps = piece // tall

    def body(where_ref, a_ref, q_ref, *refs):
        out_refs = refs[len(after) :]
        product = jnp.dot(a_ref[...], q_ref[...], preferred_element_type=F32)
        for number, out_type in enumerate(out_types):

            @pl.when(pl.program_id(0) // steps == number)
            def _(number=number, out_type=out_type):
                out_refs[number][...] = product.astype(out_type)

        for d in range(1, group):
            lanes = pl.ds(pl.multiple_of((where_ref[1] ^ d) * share, 128), share)
            out_refs[1 + d][...] = a_ref[:, lanes]

    def out_place(number):
        return pl.BlockSpec((tall, rank), lambda i, where: (jnp.clip(i - number * steps, 0, steps - 1), 0))

    def copy_row(i, where):
        return ((where[0] ^ (i // steps)) & 1) * steps + i % steps

    return pl.pallas_call(
        body,
        out_shape=[jax.ShapeDtypeStruct((piece, rank), out_type) for out_type in out_types]
        + [jax.ShapeDtypeStruct((2 * piece, share), BF16)] * (group - 1),
        grid_spec=pltpu.PrefetchScalarGridSpec(
            num_scalar_prefetch=1,
            grid=(2 * steps,),
            in_specs=[
                pl.BlockSpec((tall, columns), lambda i, where: ((where[0] ^ (i // steps)) * steps + i % steps, 0)),
                pl.BlockSpec((columns, rank), lambda i, where: (0, 0)),
            ]
            + [ANY] * len(after),
            out_specs=[out_place(0), out_place(1)]
            + [pl.BlockSpec((tall, share), lambda i, where: (copy_row(i, where), 0))] * (group - 1),
        ),
        compiler_params=params(24),
        cost_estimate=cost(4 * piece * columns * rank, piece * columns * 6),
    )(jnp.stack([piece_at, position]), accumulated, q_start, *after)


def split_sum(own, others, place, pieces):
    rows, rank = own.shape
    piece = rows // pieces

    def body(where_ref, own_ref, *refs):
        other_refs, out_refs = refs[: len(others)], refs[len(others) :]
        for d in range(pieces):
            at = pl.ds(pl.multiple_of((where_ref[0] ^ d) * piece, piece), piece)
            total = own_ref[at, :]
            for ref in other_refs:
                total += ref[at, :].astype(F32)
            out_refs[d][...] = total.astype(out_refs[d].dtype)

    return pl.pallas_call(
        body,
        out_shape=[jax.ShapeDtypeStruct((piece, rank), F32 if d == 0 else BF16) for d in range(pieces)],
        in_specs=[pl.BlockSpec(memory_space=pltpu.SMEM)] + [pl.BlockSpec(memory_space=pltpu.VMEM)] * (1 + len(others)),
        out_specs=[pl.BlockSpec(memory_space=pltpu.VMEM)] * pieces,
        compiler_params=params(24),
    )(place.reshape(1), own, *others)


def assemble(parts, place, after=()):
    rows, rank = parts[0].shape
    count = len(parts)

    def body(where_ref, *refs):
        out_ref = refs[-1]
        for d in range(count):
            at = pl.ds(pl.multiple_of((where_ref[0] ^ d) * rows, rows), rows)
            out_ref[at, :] = refs[d][...]

    return pl.pallas_call(
        body,
        out_shape=jax.ShapeDtypeStruct((rows * count, rank), parts[0].dtype),
        in_specs=[pl.BlockSpec(memory_space=pltpu.SMEM)]
        + [pl.BlockSpec(memory_space=pltpu.VMEM)] * count
        + [ANY] * len(after),
        out_specs=pl.BlockSpec(memory_space=pltpu.VMEM),
        compiler_params=params(24),
    )(place.reshape(1), *parts, *after)


def right_piece(accumulated, left, piece_at, position, shares, earlier):
    rows, columns = accumulated.shape
    piece, rank = left.shape
    share = columns // shares
    width = 896 if share % 896 == 0 else tile_width(share)
    steps = columns // width
    each = steps // shares

    def body(where_ref, a_ref, left_ref, *refs):
        out_refs, gram_ref, turned_ref = refs[len(earlier) : -2], refs[-2], refs[-1]
        at = pl.program_id(0)

        @pl.when(at == 0)
        def _():
            turned_ref[...] = left_ref[...].T
            gram_ref[...] = jnp.dot(turned_ref[...], left_ref[...], preferred_element_type=F32)

        total = jnp.dot(turned_ref[...], a_ref[...], preferred_element_type=F32)
        if earlier:
            total += refs[0][...]
        for d in range(shares):

            @pl.when(at // each == where_ref[1] ^ d)
            def _(d=d):
                out_refs[d][...] = total

    def out_place(d):
        return pl.BlockSpec((rank, width), lambda j, where: (0, jnp.clip(j - (where[1] ^ d) * each, 0, each - 1)))

    whole = pl.BlockSpec((rank, width), lambda j, where: (0, j))
    return pl.pallas_call(
        body,
        out_shape=[jax.ShapeDtypeStruct((rank, share), F32)] * shares + [jax.ShapeDtypeStruct((rank, rank), F32)],
        grid_spec=pltpu.PrefetchScalarGridSpec(
            num_scalar_prefetch=1,
            grid=(steps,),
            in_specs=[
                pl.BlockSpec((piece, width), lambda j, where: (where[0], j)),
                pl.BlockSpec((piece, rank), lambda j, where: (0, 0)),
            ]
            + [whole] * len(earlier),
            out_specs=([out_place(d) for d in range(shares)] if shares > 1 else [whole])
            + [pl.BlockSpec((rank, rank), lambda j, where: (0, 0))],
            scratch_shapes=[pltpu.VMEM((rank, piece), BF16)],
        ),
        compiler_params=params(24),
        cost_estimate=cost(2 * piece * columns * rank, piece * columns * 2),
    )(jnp.stack([piece_at, position if shares > 1 else jnp.zeros_like(position)]), accumulated, left, *earlier)


def halves(value):
    high = value.astype(BF16)
    return high, (value - high.astype(F32)).astype(BF16)


def inverse_factor(gram):
    rank = gram.shape[0]
    lane = lax.broadcasted_iota(jnp.int32, (8, rank), 1)
    row = lax.broadcasted_iota(jnp.int32, (8, rank), 0)
    left = [gram[start : start + 8, :] for start in range(0, rank, 8)]
    right = [jnp.where(lane == row + start, 1.0, 0.0).astype(F32) for start in range(0, rank, 8)]
    scales = [jnp.zeros((8, rank), F32)] * len(left)
    for k in range(rank):
        home, inside = divmod(k, 8)
        pivot_row = left[home][inside : inside + 1, :]
        pivot = left[home][inside : inside + 1, k : k + 1]
        made_row = right[home][inside : inside + 1, :]
        inverse = 1.0 / pivot
        scales[home] = jnp.where(row == inside, lax.rsqrt(jnp.broadcast_to(pivot, (8, rank))), scales[home])
        pivot_row, made_row = pivot_row * inverse, made_row * inverse
        for block in range(home, len(left)):
            if block == home and inside == 7:
                continue
            factor = jnp.broadcast_to(left[block][:, k : k + 1], (8, rank))
            if block == home:
                factor = jnp.where(row > inside, factor, 0.0)
            left[block] = left[block] - factor * pivot_row
            right[block] = right[block] - factor * made_row
    return jnp.concatenate([part * scale for part, scale in zip(right, scales)], axis=0)


def basis_of(blocks, table, position):
    group = len(blocks)
    rows, rank = blocks[0].shape
    _, count, side, _ = table.shape

    def body(*refs):
        block_refs, scale_ref, table_ref = refs[:group], refs[group], refs[group + 1]
        inverse_ref, basis_ref, basis16_ref, field_ref, turned_ref = refs[group + 2 :]

        @pl.loop(0, count, unroll=4)
        def _(b):
            at = pl.ds(pl.multiple_of(b * side, side), side)
            mixed = jnp.dot(table_ref[0, b], block_refs[0][at, :], preferred_element_type=F32)
            for d in range(1, group):
                mixed += jnp.dot(table_ref[d, b], block_refs[d][at, :], preferred_element_type=F32)
            field_ref[b] = mixed

        @pl.loop(0, side // 16, unroll=2)
        def _(i):
            inner = pl.multiple_of(i * 16, 16)
            values = butterflies([field_ref[b, pl.ds(inner, 16), :] for b in range(count)])
            for b in range(count):
                turned_ref[pl.ds(pl.multiple_of(b * side + inner, 16), 16), :] = values[b] * scale_ref[0]

        grams = [jnp.dot(ref[...].T, ref[...], preferred_element_type=F32) for ref in block_refs]
        while len(grams) > 1:
            grams = [low + high for low, high in zip(grams[::2], grams[1::2])]
        inverse = inverse_factor(grams[0])
        inverse_ref[...] = inverse
        high, low = halves(inverse.T)
        turned_high, turned_low = halves(turned_ref[...])
        both = jnp.concatenate([turned_high, turned_low], axis=1)
        basis = jnp.dot(both, jnp.concatenate([high, high], axis=0), preferred_element_type=F32)
        basis += jnp.dot(turned_high, low, preferred_element_type=F32)
        basis_ref[...] = basis
        basis16_ref[...] = basis.astype(BF16)

    return pl.pallas_call(
        body,
        out_shape=[
            jax.ShapeDtypeStruct((rank, rank), F32),
            jax.ShapeDtypeStruct((rows, rank), F32),
            jax.ShapeDtypeStruct((rows, rank), BF16),
        ],
        in_specs=[VMEM] * group + [SMEM, VMEM],
        out_specs=[VMEM] * 3,
        scratch_shapes=[pltpu.VMEM((count, side, rank), F32), pltpu.VMEM((rows, rank), F32)],
        compiler_params=params(20),
        cost_estimate=cost(8 * 10**9, 60 * 10**6),
    )(*blocks, scales_of(position, group, rows), table)


def residual(rotated, basis16, right, columns, owner, resident, into=()):
    rows, share = rotated.shape
    rank = right.shape[0]
    tall = min(512, rows)

    def body(where_ref, rotated_ref, basis_ref, right_ref, *refs):
        out_ref, factor_ref, right16_ref = refs[len(into) :]

        @pl.when(pl.program_id(0) == 0)
        def _():
            right16_ref[...] = right_ref[...].astype(BF16)
            factor_ref[...] = right_ref[...].T

        part = pl.ds(pl.multiple_of(pl.program_id(0) * tall, tall), tall) if resident else slice(None)
        for start in range(0, share, 256):
            lanes = slice(start, min(start + 256, share))
            approx = jnp.dot(basis_ref[...], right16_ref[:, lanes], preferred_element_type=F32)
            out_ref[:, lanes] = (rotated_ref[part, lanes].astype(F32) - approx).astype(out_ref.dtype)

    return pl.pallas_call(
        body,
        out_shape=[jax.ShapeDtypeStruct((rows, columns), BF16), jax.ShapeDtypeStruct((columns, rank), F32)],
        grid_spec=pltpu.PrefetchScalarGridSpec(
            num_scalar_prefetch=1,
            grid=(rows // tall,),
            in_specs=[
                VMEM if resident else pl.BlockSpec((tall, share), lambda i, where: (i, 0)),
                pl.BlockSpec((tall, rank), lambda i, where: (i, 0)),
                pl.BlockSpec((rank, share), lambda i, where: (0, 0)),
            ]
            + [ANY] * len(into),
            out_specs=[
                pl.BlockSpec((tall, share), lambda i, where: (i, where[0])),
                pl.BlockSpec((share, rank), lambda i, where: (where[0], 0)),
            ],
            scratch_shapes=[pltpu.VMEM((rank, share), BF16)],
        ),
        input_output_aliases={4: 0, 5: 1} if into else {},
        compiler_params=params(16),
        cost_estimate=cost(2 * rows * share * rank, rows * share * 2),
    )(owner.reshape(1), rotated, basis16, right, *into)


def from_distance(block, axis, distance):
    count = lax.axis_size(axis)
    return lax.ppermute(block, axis, [(p, p ^ distance) for p in range(count)])


def from_plane(block, distance):
    count, mp_count = REPLICAS * lax.axis_size("mp"), lax.axis_size("mp")
    change = (distance & 1) | (distance >> 1) * mp_count
    return lax.ppermute(block, ("rep", "mp"), [(p, p ^ change) for p in range(count)])


def from_line(block, distance):
    return from_distance(block, "mp", distance << 1)


def local(accumulated, signs, q_start):
    rows, columns = accumulated.shape
    rank = q_start.shape[1]
    group = lax.axis_size("pos")
    position = lax.axis_index("pos")
    mp_index = lax.axis_index("mp")
    plane = lax.axis_index("rep") * 2 + (mp_index & 1)
    line, lines = mp_index >> 1, lax.axis_size("mp") // 2
    share = columns // group
    shared = share % 128 == 0 and rows % (256 * PLANE) == 0
    others = range(1, group)

    came, after = [], ()
    other_pieces = [[] for _ in others]
    for d in (3, 1):
        out_types = (BF16, BF16 if d > 1 else F32)
        first, second, *copies = project(
            accumulated, q_start, plane ^ d, position, group if shared else 1, out_types, after
        )
        after = (second,)
        came.append(from_plane(first, d))
        if d > 1:
            came.append(from_plane(second, d - 1))
        for e, copy in enumerate(copies):
            other_pieces[e].append(from_distance(copy, "pos", e + 1))
    table = signed_hadamard(signs, position, group, rows)
    if not shared:
        other_pieces = [[from_distance(accumulated, "pos", d)] for d in others]
    blocks = [[accumulated]] + other_pieces

    own, *sent = split_sum(second, came, line, lines)
    came = [from_line(sent[d - 1], d) for d in range(1, lines)]
    mine16 = sum([part.astype(F32) for part in came], own).astype(BF16)
    near16 = assemble([mine16] + [from_line(mine16, d) for d in range(1, lines)], line)
    far16 = [near16] + [from_plane(near16, d) for d in range(1, PLANE)]
    own16 = assemble(far16, plane)
    around16 = [own16] + [from_distance(own16, "pos", d) for d in others]

    if shared:
        *rotated, half = rotate_and_right(blocks, table, around16, position, plane)
        half = half.astype(BF16)
        rotated = rotated[:1] + [from_distance(part, "pos", d + 1) for d, part in enumerate(rotated[1:])]
        half = half.astype(F32) + from_distance(half, "rep", 1).astype(F32)
    else:
        rotated = rotate(blocks, table, position, plane, BF16, 1)
        totals = []
        for d in range(PLANE):
            *totals, _ = right_piece(accumulated, far16[d], plane ^ d, position, 1, totals)
        half = lax.psum(totals[0], ("rep", "pos"))
    inverse, p_basis, basis16 = basis_of(around16, table, position)

    right = jnp.dot(inverse, half, precision=lax.Precision.HIGHEST) / REPLICAS
    if not shared:
        new_error, q_factor = residual(rotated[0], basis16, right, columns, jnp.zeros((), jnp.int32), False)
        return (new_error, p_basis, q_factor)
    rights = [right] + [from_distance(right, "pos", d) for d in others]
    results = ()
    for d in range(group):
        results = residual(rotated[d], basis16, rights[d], columns, position ^ d, d == 0, results)
    new_error, q_factor = results
    return (new_error, p_basis, q_factor)


def solution(mesh):
    dp_count, mp_count = mesh.shape["dp"], mesh.shape["mp"]
    fine = Mesh(
        mesh.devices.reshape(REPLICAS, dp_count // REPLICAS, mp_count), ("rep", "pos", "mp")
    )
    rows_of = ("rep", "pos")
    in_specs = (P(rows_of, "mp"), P(), P("mp", None))
    out_specs = (P(rows_of, "mp"), P(rows_of, None), P("mp", None))
    return jax.shard_map(local, mesh=fine, in_specs=in_specs, out_specs=out_specs, check_vma=False)
```

```python
import functools
import math

import jax
import jax.numpy as jnp
from jax import lax
from jax.experimental import pallas as pl
from jax.experimental.pallas import tpu as pltpu
from jax.sharding import Mesh, PartitionSpec as P

REPLICAS = 2
PLANE = 2 * REPLICAS
F32 = jnp.float32
BF16 = jnp.bfloat16
ANY = pl.BlockSpec(memory_space=pl.ANY)
VMEM = pl.BlockSpec(memory_space=pltpu.VMEM)
SMEM = pl.BlockSpec(memory_space=pltpu.SMEM)
MIB = 1024 * 1024


def cost(flops, size):
    return pl.CostEstimate(flops=flops, bytes_accessed=size, transcendentals=0)


def params(mib):
    return pltpu.CompilerParams(vmem_limit_bytes=mib * MIB)


def sylvester(size):
    index = jnp.arange(size, dtype=jnp.int32)
    parity = lax.population_count(index[:, None] & index[None, :]) & 1
    return (1 - 2 * parity).astype(F32)


def butterflies(values):
    values = list(values)
    step = 1
    while step < len(values):
        for low in range(len(values)):
            if not low & step:
                high = low | step
                values[low], values[high] = values[low] + values[high], values[low] - values[high]
        step *= 2
    return values


def tile_width(columns):
    return 256 if columns % 256 == 0 else 128


def minus_one_to(number):
    return 1 - 2 * (lax.population_count(number) & 1)


def signed_hadamard(signs, position, group, rows):
    side = min(256, rows)
    parts = []
    for distance in range(group):
        mine = lax.dynamic_slice_in_dim(signs, (position ^ distance) * rows, rows)
        parts.append((2 * mine - 1) * minus_one_to(position & distance))
    flips = jnp.stack(parts).astype(F32).reshape(group, rows // side, 1, side)
    return (sylvester(side) * flips).astype(BF16)


def rotate_body(group, outs, pieces, *refs):
    where_ref, refs = refs[0], refs[1:]
    total = sum(pieces)
    block_refs, at = [], 0
    for number in pieces:
        block_refs.append(refs[at : at + number])
        at += number
    scale_ref, table_ref = refs[total], refs[total + 1]
    fields = 2 if pl.num_programs(0) > 1 else 1
    out_refs, field_refs = refs[-fields - outs : -fields], refs[-fields:]
    _, count, side, width = field_refs[0].shape
    cuts = PLANE if max(pieces) > 1 else 1
    each = count // cuts
    strip = side // count

    def mix(e, inside, field_ref):
        b = (where_ref[1] ^ e) * each + inside
        parts = []
        for d in range(group):
            if pieces[d] > 1:
                array, part = divmod(PLANE - 1 - e, PLANE // pieces[d])
                ref, first = block_refs[d][array], (part * each + inside) * side
            else:
                ref, first = block_refs[d][0], b * side
            rows = pl.ds(pl.multiple_of(first, side), side)
            parts.append(jnp.dot(table_ref[d, b], ref[rows, :], preferred_element_type=F32))
        mixed = butterflies(parts) if outs > 1 else [sum(parts[1:], parts[0])]
        for o in range(outs):
            field_ref[o, b] = mixed[o]

    def spread(i, field_ref):
        for part in range(0, strip, 16):
            inner = pl.multiple_of(i * strip + part, 16)
            for o in range(outs):
                for start in range(0, width, 128):
                    lanes = slice(start, start + 128)
                    values = butterflies([field_ref[o, b, pl.ds(inner, 16), lanes] for b in range(count)])
                    for b in range(count):
                        turned = (values[b] * scale_ref[o]).astype(out_refs[o].dtype)
                        out_refs[o][pl.ds(pl.multiple_of(b * side + inner, 16), 16), lanes] = turned

    def sweep(mixed_ref, spread_ref):
        for e in range(cuts):

            @pl.loop(0, each, unroll=2)
            def _(inside, e=e):
                if mixed_ref is not None:
                    mix(e, inside, mixed_ref)
                if spread_ref is not None:
                    spread(e * each + inside, spread_ref)

    if fields == 1:
        sweep(field_refs[0], None)
        sweep(None, field_refs[0])
        return
    odd = pl.program_id(0) % 2 == 1

    @pl.when(jnp.logical_not(odd))
    def _():
        sweep(field_refs[0], field_refs[1])

    @pl.when(odd)
    def _():
        sweep(field_refs[1], field_refs[0])


def rotate(blocks, table, position, plane, out_type, outs, first=0, steps=None, after=()):
    group = len(blocks)
    pieces = [len(block) for block in blocks]
    rows = sum(piece.shape[0] for piece in blocks[0])
    columns = blocks[-1][0].shape[1]
    _, count, side, _ = table.shape
    width = tile_width(columns)
    tiles = columns // width
    steps = tiles if steps is None else steps
    distances = jnp.arange(group, dtype=jnp.int32)
    scales = (minus_one_to(position) * minus_one_to(position & distances)).astype(F32) / math.sqrt(rows * group)
    where = jnp.stack([position, plane if max(pieces) > 1 else jnp.zeros_like(plane)])

    fields = 2 if steps > 1 else 1

    def place(piece):
        def index(j, where):
            j = first + jnp.minimum(j, steps - 1)
            return 0, j if piece.shape[1] == columns else where[0] * tiles + j

        return pl.BlockSpec((piece.shape[0], width), index)

    flat = [piece for block in blocks for piece in block]
    kept = 1 + len(flat) + 2

    def body(*refs):
        rotate_body(group, outs, pieces, *refs[:kept], *refs[kept + len(after) :])

    size = rows * steps * width
    return pl.pallas_call(
        body,
        out_shape=[jax.ShapeDtypeStruct((rows, steps * width), out_type)] * outs,
        grid_spec=pltpu.PrefetchScalarGridSpec(
            num_scalar_prefetch=1,
            grid=(steps + fields - 1,),
            in_specs=[place(piece) for piece in flat]
            + [pl.BlockSpec(memory_space=pltpu.SMEM), pl.BlockSpec(table.shape, lambda j, where: (0, 0, 0, 0))]
            + [ANY] * len(after),
            out_specs=[pl.BlockSpec((rows, width), lambda j, where: (0, jnp.maximum(j - (fields - 1), 0)))] * outs,
            scratch_shapes=[pltpu.VMEM((outs, count, side, width), F32)] * fields,
        ),
        compiler_params=params(24),
        cost_estimate=cost(2 * size * side * group, size * 2 * (group + outs) + table.size * 2),
    )(where, *flat, scales, table, *after)


def scales_of(position, group, rows):
    distances = jnp.arange(group, dtype=jnp.int32)
    return (minus_one_to(position) * minus_one_to(position & distances)).astype(F32) / math.sqrt(rows * group)


def rotate_and_right(blocks, table, lefts, position, plane):
    group = len(blocks)
    pieces = [len(block) for block in blocks]
    rows = blocks[0][0].shape[0]
    rank = lefts[0].shape[1]
    columns = blocks[-1][0].shape[1]
    _, count, side, _ = table.shape
    width = tile_width(columns)
    tiles = columns // width
    each = count // PLANE
    strip = side // count
    where = jnp.stack([position, plane >> 1])

    def body(where_ref, *refs):
        at, block_refs = 0, []
        for number in pieces:
            block_refs.append(refs[at : at + number])
            at += number
        scale_ref, table_ref = refs[at : at + 2]
        left_refs, out_refs = refs[at + 2 : at + 2 + group], refs[at + 2 + group : at + 2 + 2 * group]
        right_ref, even_ref, odd_ref, both_ref, total_ref = refs[-5:]
        step = pl.program_id(0)
        shown = jnp.maximum(step - 1, 0) * width

        def block_rows(d, number, first, size):
            if pieces[d] > 1:
                return block_refs[d][1 - number][pl.ds(first, size), :]
            pair = rows // 2
            start = pl.multiple_of((where_ref[1] ^ number) * pair + first, side)
            return block_refs[d][0][pl.ds(start, size), :]

        def mix(number, inside, field_ref):
            b = (where_ref[1] ^ number) * (count // 2) + inside
            first = pl.multiple_of(inside * side, side)
            products = [
                jnp.dot(both_ref[d, b], block_rows(d, number, first, side), preferred_element_type=F32)
                for d in range(group)
            ]
            total_ref[...] += sum([product[side:] for product in products[1:]], products[0][side:])
            for o, mixed in enumerate(butterflies([product[:side] for product in products])):
                field_ref[o, b] = mixed

        def spread(i, field_ref):
            for part in range(0, strip, 16):
                inner = pl.multiple_of(i * strip + part, 16)
                for o in range(group):
                    for start in range(0, width, 128):
                        lanes = slice(start, start + 128)
                        values = butterflies([field_ref[o, b, pl.ds(inner, 16), lanes] for b in range(count)])
                        if o == 0:
                            lanes = pl.ds(pl.multiple_of(shown + start, 128), 128)
                        for b in range(count):
                            turned = (values[b] * scale_ref[o]).astype(BF16)
                            out_refs[o][pl.ds(pl.multiple_of(b * side + inner, 16), 16), lanes] = turned

        def sweep(mixed_ref, spread_ref):
            for number in range(2):

                @pl.loop(0, count // 2, unroll=2)
                def _(inside, number=number):
                    if mixed_ref is not None:
                        mix(number, inside, mixed_ref)
                    if spread_ref is not None:
                        spread(number * (count // 2) + inside, spread_ref)

        @pl.when(step == 0)
        def _():
            for d in range(group):
                for b in range(count):
                    both_ref[d, b, :side, :] = table_ref[d, b]
                    both_ref[d, b, side:, :] = left_refs[d][b * side : (b + 1) * side, :].T

        @pl.when(step < tiles)
        def _():
            total_ref[...] = jnp.zeros_like(total_ref)

        fields = (even_ref, odd_ref)

        @pl.when(step == 0)
        def _():
            sweep(fields[0], None)

        for parity in range(2):

            @pl.when((step > 0) & (step < tiles) & (step % 2 == parity))
            def _(parity=parity):
                sweep(fields[parity], fields[1 - parity])

        @pl.when(step < tiles)
        def _():
            right_ref[...] = total_ref[...].astype(BF16)

        @pl.when(step == tiles)
        def _():
            sweep(None, fields[(tiles - 1) % 2])

    def place(piece):
        def index(j, where):
            j = jnp.minimum(j, tiles - 1)
            return 0, j if piece.shape[1] == columns else where[0] * tiles + j

        return pl.BlockSpec((piece.shape[0], width), index)

    flat = [piece for block in blocks for piece in block]
    field = pltpu.VMEM((group, count, side, width), F32)
    size = rows * columns
    return pl.pallas_call(
        body,
        out_shape=[pltpu.VMEM((rows, columns), BF16)]
        + [jax.ShapeDtypeStruct((rows, columns), BF16)] * (group - 1)
        + [jax.ShapeDtypeStruct((rank, columns), BF16)],
        grid_spec=pltpu.PrefetchScalarGridSpec(
            num_scalar_prefetch=1,
            grid=(tiles + 1,),
            in_specs=[place(piece) for piece in flat] + [SMEM, VMEM] + [VMEM] * group,
            out_specs=[VMEM]
            + [pl.BlockSpec((rows, width), lambda j, where: (0, jnp.maximum(j - 1, 0)))] * (group - 1)
            + [pl.BlockSpec((rank, width), lambda j, where: (0, jnp.minimum(j, tiles - 1)))],
            scratch_shapes=[
                field,
                field,
                pltpu.VMEM((group, count, side + rank, side), BF16),
                pltpu.VMEM((rank, width), F32),
            ],
        ),
        compiler_params=params(41),
        cost_estimate=cost(2 * size * (side + rank) * group, size * 2 * (2 * group - 1) + table.size * 2),
    )(where, *flat, scales_of(position, group, rows), table, *lefts)


def project(accumulated, q_start, piece_at, position, group, out_types, after, copies=()):
    rows, columns = accumulated.shape
    rank = q_start.shape[1]
    share = columns // group
    piece = rows // PLANE
    tall = min(512, piece)
    steps = piece // tall

    def body(where_ref, a_ref, q_ref, *refs):
        out_refs = refs[len(after) + len(copies) :]
        product = jnp.dot(a_ref[...], q_ref[...], preferred_element_type=F32)
        for number, out_type in enumerate(out_types):

            @pl.when(pl.program_id(0) // steps == number)
            def _(number=number, out_type=out_type):
                out_refs[number][...] = product.astype(out_type)

        for d in range(1, group):
            lanes = pl.ds(pl.multiple_of((where_ref[1] ^ d) * share, 128), share)
            out_refs[len(out_types) + d - 1][...] = a_ref[:, lanes]

    def out_place(number):
        return pl.BlockSpec((tall, rank), lambda i, where: (jnp.clip(i - number * steps, 0, steps - 1), 0))

    def copy_row(i, where):
        return ((where[0] ^ (i // steps)) & 1) * steps + i % steps

    return pl.pallas_call(
        body,
        out_shape=[jax.ShapeDtypeStruct((piece, rank), out_type) for out_type in out_types]
        + [jax.ShapeDtypeStruct((2 * piece, share), BF16)] * (group - 1),
        grid_spec=pltpu.PrefetchScalarGridSpec(
            num_scalar_prefetch=1,
            grid=(len(out_types) * steps,),
            in_specs=[
                pl.BlockSpec((tall, columns), lambda i, where: ((where[0] ^ (i // steps)) * steps + i % steps, 0)),
                pl.BlockSpec((columns, rank), lambda i, where: (0, 0)),
            ]
            + [ANY] * (len(after) + len(copies)),
            out_specs=[out_place(number) for number in range(len(out_types))]
            + [pl.BlockSpec((tall, share), lambda i, where: (copy_row(i, where), 0))] * (group - 1),
        ),
        input_output_aliases={3 + len(after) + d: len(out_types) + d for d in range(len(copies))},
        compiler_params=params(24),
        cost_estimate=cost(2 * len(out_types) * piece * columns * rank, len(out_types) * piece * columns * 3),
    )(jnp.stack([piece_at, position]), accumulated, q_start, *after, *copies)


def split_sum(own, others, place, pieces):
    rows, rank = own.shape
    piece = rows // pieces

    def body(where_ref, own_ref, *refs):
        other_refs, out_refs = refs[: len(others)], refs[len(others) :]
        for d in range(pieces):
            at = pl.ds(pl.multiple_of((where_ref[0] ^ d) * piece, piece), piece)
            total = own_ref[at, :]
            for ref in other_refs:
                total += ref[at, :].astype(F32)
            out_refs[d][...] = total.astype(out_refs[d].dtype)

    return pl.pallas_call(
        body,
        out_shape=[jax.ShapeDtypeStruct((piece, rank), F32 if d == 0 else BF16) for d in range(pieces)],
        in_specs=[pl.BlockSpec(memory_space=pltpu.SMEM)] + [pl.BlockSpec(memory_space=pltpu.VMEM)] * (1 + len(others)),
        out_specs=[pl.BlockSpec(memory_space=pltpu.VMEM)] * pieces,
        compiler_params=params(24),
    )(place.reshape(1), own, *others)


def assemble(parts, place, after=()):
    rows, rank = parts[0].shape
    count = len(parts)

    def body(where_ref, *refs):
        out_ref = refs[-1]
        for d in range(count):
            at = pl.ds(pl.multiple_of((where_ref[0] ^ d) * rows, rows), rows)
            out_ref[at, :] = refs[d][...]

    return pl.pallas_call(
        body,
        out_shape=jax.ShapeDtypeStruct((rows * count, rank), parts[0].dtype),
        in_specs=[pl.BlockSpec(memory_space=pltpu.SMEM)]
        + [pl.BlockSpec(memory_space=pltpu.VMEM)] * count
        + [ANY] * len(after),
        out_specs=pl.BlockSpec(memory_space=pltpu.VMEM),
        compiler_params=params(24),
    )(place.reshape(1), *parts, *after)


def right_piece(accumulated, left, piece_at, position, shares, earlier):
    rows, columns = accumulated.shape
    piece, rank = left.shape
    share = columns // shares
    width = 896 if share % 896 == 0 else tile_width(share)
    steps = columns // width
    each = steps // shares

    def body(where_ref, a_ref, left_ref, *refs):
        out_refs, gram_ref, turned_ref = refs[len(earlier) : -2], refs[-2], refs[-1]
        at = pl.program_id(0)

        @pl.when(at == 0)
        def _():
            turned_ref[...] = left_ref[...].T
            gram_ref[...] = jnp.dot(turned_ref[...], left_ref[...], preferred_element_type=F32)

        total = jnp.dot(turned_ref[...], a_ref[...], preferred_element_type=F32)
        if earlier:
            total += refs[0][...]
        for d in range(shares):

            @pl.when(at // each == where_ref[1] ^ d)
            def _(d=d):
                out_refs[d][...] = total

    def out_place(d):
        return pl.BlockSpec((rank, width), lambda j, where: (0, jnp.clip(j - (where[1] ^ d) * each, 0, each - 1)))

    whole = pl.BlockSpec((rank, width), lambda j, where: (0, j))
    return pl.pallas_call(
        body,
        out_shape=[jax.ShapeDtypeStruct((rank, share), F32)] * shares + [jax.ShapeDtypeStruct((rank, rank), F32)],
        grid_spec=pltpu.PrefetchScalarGridSpec(
            num_scalar_prefetch=1,
            grid=(steps,),
            in_specs=[
                pl.BlockSpec((piece, width), lambda j, where: (where[0], j)),
                pl.BlockSpec((piece, rank), lambda j, where: (0, 0)),
            ]
            + [whole] * len(earlier),
            out_specs=([out_place(d) for d in range(shares)] if shares > 1 else [whole])
            + [pl.BlockSpec((rank, rank), lambda j, where: (0, 0))],
            scratch_shapes=[pltpu.VMEM((rank, piece), BF16)],
        ),
        compiler_params=params(24),
        cost_estimate=cost(2 * piece * columns * rank, piece * columns * 2),
    )(jnp.stack([piece_at, position if shares > 1 else jnp.zeros_like(position)]), accumulated, left, *earlier)


def halves(value):
    high = value.astype(BF16)
    return high, (value - high.astype(F32)).astype(BF16)


def inverse_factor(gram):
    rank = gram.shape[0]
    lane = lax.broadcasted_iota(jnp.int32, (8, rank), 1)
    row = lax.broadcasted_iota(jnp.int32, (8, rank), 0)
    left = [gram[start : start + 8, :] for start in range(0, rank, 8)]
    right = [jnp.where(lane == row + start, 1.0, 0.0).astype(F32) for start in range(0, rank, 8)]
    scales = [jnp.zeros((8, rank), F32)] * len(left)
    for k in range(rank):
        home, inside = divmod(k, 8)
        pivot_row = left[home][inside : inside + 1, :]
        pivot = left[home][inside : inside + 1, k : k + 1]
        made_row = right[home][inside : inside + 1, :]
        root = lax.rsqrt(jnp.broadcast_to(pivot, (1, rank)))
        scales[home] = jnp.where(row == inside, root, scales[home])
        pivot_row, made_row = pivot_row * root * root, made_row * root * root
        for block in range(home, len(left)):
            if block == home and inside == 7:
                continue
            factor = jnp.broadcast_to(left[block][:, k : k + 1], (8, rank))
            if block == home:
                factor = jnp.where(row > inside, factor, 0.0)
            left[block] = left[block] - factor * pivot_row
            right[block] = right[block] - factor * made_row
    return jnp.concatenate([part * scale for part, scale in zip(right, scales)], axis=0)


def basis_of(blocks, table, position):
    group = len(blocks)
    rows, rank = blocks[0].shape
    _, count, side, _ = table.shape

    def body(*refs):
        block_refs, scale_ref, table_ref = refs[:group], refs[group], refs[group + 1]
        inverse_ref, basis_ref, basis16_ref, field_ref, turned_ref = refs[group + 2 :]

        @pl.loop(0, count, unroll=4)
        def _(b):
            at = pl.ds(pl.multiple_of(b * side, side), side)
            mixed = jnp.dot(table_ref[0, b], block_refs[0][at, :], preferred_element_type=F32)
            for d in range(1, group):
                mixed += jnp.dot(table_ref[d, b], block_refs[d][at, :], preferred_element_type=F32)
            field_ref[b] = mixed

        @pl.loop(0, side // 16, unroll=2)
        def _(i):
            inner = pl.multiple_of(i * 16, 16)
            values = butterflies([field_ref[b, pl.ds(inner, 16), :] for b in range(count)])
            for b in range(count):
                turned_ref[pl.ds(pl.multiple_of(b * side + inner, 16), 16), :] = values[b] * scale_ref[0]

        grams = [jnp.dot(ref[...].T, ref[...], preferred_element_type=F32) for ref in block_refs]
        while len(grams) > 1:
            grams = [low + high for low, high in zip(grams[::2], grams[1::2])]
        inverse = inverse_factor(grams[0])
        inverse_ref[...] = inverse
        high, low = halves(inverse.T)
        turned_high, turned_low = halves(turned_ref[...])
        both = jnp.concatenate([turned_high, turned_low], axis=1)
        basis = jnp.dot(both, jnp.concatenate([high, high], axis=0), preferred_element_type=F32)
        basis += jnp.dot(turned_high, low, preferred_element_type=F32)
        basis_ref[...] = basis
        basis16_ref[...] = basis.astype(BF16)

    return pl.pallas_call(
        body,
        out_shape=[
            jax.ShapeDtypeStruct((rank, rank), F32),
            jax.ShapeDtypeStruct((rows, rank), F32),
            jax.ShapeDtypeStruct((rows, rank), BF16),
        ],
        in_specs=[VMEM] * group + [SMEM, VMEM],
        out_specs=[VMEM] * 3,
        scratch_shapes=[pltpu.VMEM((count, side, rank), F32), pltpu.VMEM((rows, rank), F32)],
        compiler_params=params(10),
        cost_estimate=cost(8 * 10**9, 60 * 10**6),
    )(*blocks, scales_of(position, group, rows), table)


def residual(rotated, basis16, right, columns, owner, resident, into=()):
    rows, share = rotated.shape
    rank = right.shape[0]
    tall = min(512, rows)

    def body(where_ref, rotated_ref, basis_ref, right_ref, *refs):
        out_ref, factor_ref, right16_ref = refs[len(into) :]

        @pl.when(pl.program_id(0) == 0)
        def _():
            right16_ref[...] = right_ref[...].astype(BF16)
            factor_ref[...] = right_ref[...].T

        part = pl.ds(pl.multiple_of(pl.program_id(0) * tall, tall), tall) if resident else slice(None)
        for start in range(0, share, 256):
            lanes = slice(start, min(start + 256, share))
            approx = jnp.dot(basis_ref[...], right16_ref[:, lanes], preferred_element_type=F32)
            out_ref[:, lanes] = (rotated_ref[part, lanes].astype(F32) - approx).astype(out_ref.dtype)

    return pl.pallas_call(
        body,
        out_shape=[jax.ShapeDtypeStruct((rows, columns), BF16), jax.ShapeDtypeStruct((columns, rank), F32)],
        grid_spec=pltpu.PrefetchScalarGridSpec(
            num_scalar_prefetch=1,
            grid=(rows // tall,),
            in_specs=[
                VMEM if resident else pl.BlockSpec((tall, share), lambda i, where: (i, 0)),
                pl.BlockSpec((tall, rank), lambda i, where: (i, 0)),
                pl.BlockSpec((rank, share), lambda i, where: (0, 0)),
            ]
            + [ANY] * len(into),
            out_specs=[
                pl.BlockSpec((tall, share), lambda i, where: (i, where[0])),
                pl.BlockSpec((share, rank), lambda i, where: (where[0], 0)),
            ],
            scratch_shapes=[pltpu.VMEM((rank, share), BF16)],
        ),
        input_output_aliases={4: 0, 5: 1} if into else {},
        compiler_params=params(10),
        cost_estimate=cost(2 * rows * share * rank, rows * share * 2),
    )(owner.reshape(1), rotated, basis16, right, *into)


def from_distance(block, axis, distance):
    count = lax.axis_size(axis)
    return lax.ppermute(block, axis, [(p, p ^ distance) for p in range(count)])


def from_plane(block, distance):
    count, mp_count = REPLICAS * lax.axis_size("mp"), lax.axis_size("mp")
    change = (distance & 1) | (distance >> 1) * mp_count
    return lax.ppermute(block, ("rep", "mp"), [(p, p ^ change) for p in range(count)])


def from_line(block, distance):
    return from_distance(block, "mp", distance << 1)


def local(accumulated, signs, q_start):
    rows, columns = accumulated.shape
    rank = q_start.shape[1]
    group = lax.axis_size("pos")
    position = lax.axis_index("pos")
    mp_index = lax.axis_index("mp")
    plane = lax.axis_index("rep") * 2 + (mp_index & 1)
    line, lines = mp_index >> 1, lax.axis_size("mp") // 2
    share = columns // group
    shared = share % 128 == 0 and rows % (256 * PLANE) == 0
    others = range(1, group)

    came, after, copies = [], (), ()
    other_pieces = [[] for _ in others]
    for sent in ((3,), (2,), (1,), (0,)):
        out_types = [BF16 if d else F32 for d in sent]
        results = project(
            accumulated, q_start, plane ^ sent[0], position, group if shared else 1, out_types, after, copies
        )
        parts, copies = results[: len(sent)], tuple(results[len(sent) :])
        after = (parts[-1],)
        came += [from_plane(part, d) for part, d in zip(parts, sent) if d]
        if sent[0] == 1:
            after += (came[0],)
        if sent[0] % 2 == 0:
            for e, copy in enumerate(copies):
                other_pieces[e].append(from_distance(copy, "pos", e + 1))
            copies = ()
    table = signed_hadamard(signs, position, group, rows)
    if not shared:
        other_pieces = [[from_distance(accumulated, "pos", d)] for d in others]
    blocks = [[accumulated]] + other_pieces

    own, *sent = split_sum(parts[0], came, line, lines)
    came = [from_line(sent[d - 1], d) for d in range(1, lines)]
    mine16 = sum([part.astype(F32) for part in came], own).astype(BF16)
    near16 = assemble([mine16] + [from_line(mine16, d) for d in range(1, lines)], line)
    far16 = [near16] + [from_plane(near16, d) for d in range(1, PLANE)]
    own16 = assemble(far16, plane)
    around16 = [own16] + [from_distance(own16, "pos", d) for d in others]

    if shared:
        *rotated, half = rotate_and_right(blocks, table, around16, position, plane)
        rotated = rotated[:1] + [from_distance(part, "pos", d + 1) for d, part in enumerate(rotated[1:])]
        half = half.astype(F32) + from_distance(half, "rep", 1).astype(F32)
    else:
        rotated = rotate(blocks, table, position, plane, BF16, 1)
        totals = []
        for d in range(PLANE):
            *totals, _ = right_piece(accumulated, far16[d], plane ^ d, position, 1, totals)
        half = lax.psum(totals[0], ("rep", "pos"))
    inverse, p_basis, basis16 = basis_of(around16, table, position)

    right = jnp.dot(inverse, half, precision=lax.Precision.HIGHEST) / REPLICAS
    if not shared:
        new_error, q_factor = residual(rotated[0], basis16, right, columns, jnp.zeros((), jnp.int32), False)
        return (new_error, p_basis, q_factor)
    rights = [right] + [from_distance(right, "pos", d) for d in others]
    results = ()
    for d in range(group):
        results = residual(rotated[d], basis16, rights[d], columns, position ^ d, d == 0, results)
    new_error, q_factor = results
    return (new_error, p_basis, q_factor)


def solution(mesh):
    dp_count, mp_count = mesh.shape["dp"], mesh.shape["mp"]
    fine = Mesh(
        mesh.devices.reshape(REPLICAS, dp_count // REPLICAS, mp_count), ("rep", "pos", "mp")
    )
    rows_of = ("rep", "pos")
    in_specs = (P(rows_of, "mp"), P(), P("mp", None))
    out_specs = (P(rows_of, "mp"), P(rows_of, None), P("mp", None))
    return jax.shard_map(local, mesh=fine, in_specs=in_specs, out_specs=out_specs, check_vma=False)
```

```python
import functools
import math

import jax
import jax.numpy as jnp
from jax import lax
from jax.experimental import pallas as pl
from jax.experimental.pallas import tpu as pltpu
from jax.sharding import Mesh, PartitionSpec as P

REPLICAS = 2
PLANE = 2 * REPLICAS
F32 = jnp.float32
BF16 = jnp.bfloat16
ANY = pl.BlockSpec(memory_space=pl.ANY)
VMEM = pl.BlockSpec(memory_space=pltpu.VMEM)
SMEM = pl.BlockSpec(memory_space=pltpu.SMEM)
MIB = 1024 * 1024


def cost(flops, size):
    return pl.CostEstimate(flops=flops, bytes_accessed=size, transcendentals=0)


def params(mib):
    return pltpu.CompilerParams(vmem_limit_bytes=mib * MIB)


def sylvester(size):
    index = jnp.arange(size, dtype=jnp.int32)
    parity = lax.population_count(index[:, None] & index[None, :]) & 1
    return (1 - 2 * parity).astype(F32)


def butterflies(values):
    values = list(values)
    step = 1
    while step < len(values):
        for low in range(len(values)):
            if not low & step:
                high = low | step
                values[low], values[high] = values[low] + values[high], values[low] - values[high]
        step *= 2
    return values


def tile_width(columns):
    return 256 if columns % 256 == 0 else 128


def minus_one_to(number):
    return 1 - 2 * (lax.population_count(number) & 1)


def signed_hadamard(signs, position, group, rows):
    side = min(256, rows)
    parts = []
    for distance in range(group):
        mine = lax.dynamic_slice_in_dim(signs, (position ^ distance) * rows, rows)
        parts.append((2 * mine - 1) * minus_one_to(position & distance))
    flips = jnp.stack(parts).astype(F32).reshape(group, rows // side, 1, side)
    return (sylvester(side) * flips).astype(BF16)


def rotate_body(group, outs, pieces, *refs):
    where_ref, refs = refs[0], refs[1:]
    total = sum(pieces)
    block_refs, at = [], 0
    for number in pieces:
        block_refs.append(refs[at : at + number])
        at += number
    scale_ref, table_ref = refs[total], refs[total + 1]
    fields = 2 if pl.num_programs(0) > 1 else 1
    out_refs, field_refs = refs[-fields - outs : -fields], refs[-fields:]
    _, count, side, width = field_refs[0].shape
    cuts = PLANE if max(pieces) > 1 else 1
    each = count // cuts
    strip = side // count

    def mix(e, inside, field_ref):
        b = (where_ref[1] ^ e) * each + inside
        parts = []
        for d in range(group):
            if pieces[d] > 1:
                array, part = divmod(PLANE - 1 - e, PLANE // pieces[d])
                ref, first = block_refs[d][array], (part * each + inside) * side
            else:
                ref, first = block_refs[d][0], b * side
            rows = pl.ds(pl.multiple_of(first, side), side)
            parts.append(jnp.dot(table_ref[d, b], ref[rows, :], preferred_element_type=F32))
        mixed = butterflies(parts) if outs > 1 else [sum(parts[1:], parts[0])]
        for o in range(outs):
            field_ref[o, b] = mixed[o]

    def spread(i, field_ref):
        for part in range(0, strip, 16):
            inner = pl.multiple_of(i * strip + part, 16)
            for o in range(outs):
                for start in range(0, width, 128):
                    lanes = slice(start, start + 128)
                    values = butterflies([field_ref[o, b, pl.ds(inner, 16), lanes] for b in range(count)])
                    for b in range(count):
                        turned = (values[b] * scale_ref[o]).astype(out_refs[o].dtype)
                        out_refs[o][pl.ds(pl.multiple_of(b * side + inner, 16), 16), lanes] = turned

    def sweep(mixed_ref, spread_ref):
        for e in range(cuts):

            @pl.loop(0, each, unroll=2)
            def _(inside, e=e):
                if mixed_ref is not None:
                    mix(e, inside, mixed_ref)
                if spread_ref is not None:
                    spread(e * each + inside, spread_ref)

    if fields == 1:
        sweep(field_refs[0], None)
        sweep(None, field_refs[0])
        return
    odd = pl.program_id(0) % 2 == 1

    @pl.when(jnp.logical_not(odd))
    def _():
        sweep(field_refs[0], field_refs[1])

    @pl.when(odd)
    def _():
        sweep(field_refs[1], field_refs[0])


def rotate(blocks, table, position, plane, out_type, outs, first=0, steps=None, after=()):
    group = len(blocks)
    pieces = [len(block) for block in blocks]
    rows = sum(piece.shape[0] for piece in blocks[0])
    columns = blocks[-1][0].shape[1]
    _, count, side, _ = table.shape
    width = tile_width(columns)
    tiles = columns // width
    steps = tiles if steps is None else steps
    distances = jnp.arange(group, dtype=jnp.int32)
    scales = (minus_one_to(position) * minus_one_to(position & distances)).astype(F32) / math.sqrt(rows * group)
    where = jnp.stack([position, plane if max(pieces) > 1 else jnp.zeros_like(plane)])

    fields = 2 if steps > 1 else 1

    def place(piece):
        def index(j, where):
            j = first + jnp.minimum(j, steps - 1)
            return 0, j if piece.shape[1] == columns else where[0] * tiles + j

        return pl.BlockSpec((piece.shape[0], width), index)

    flat = [piece for block in blocks for piece in block]
    kept = 1 + len(flat) + 2

    def body(*refs):
        rotate_body(group, outs, pieces, *refs[:kept], *refs[kept + len(after) :])

    size = rows * steps * width
    return pl.pallas_call(
        body,
        out_shape=[jax.ShapeDtypeStruct((rows, steps * width), out_type)] * outs,
        grid_spec=pltpu.PrefetchScalarGridSpec(
            num_scalar_prefetch=1,
            grid=(steps + fields - 1,),
            in_specs=[place(piece) for piece in flat]
            + [pl.BlockSpec(memory_space=pltpu.SMEM), pl.BlockSpec(table.shape, lambda j, where: (0, 0, 0, 0))]
            + [ANY] * len(after),
            out_specs=[pl.BlockSpec((rows, width), lambda j, where: (0, jnp.maximum(j - (fields - 1), 0)))] * outs,
            scratch_shapes=[pltpu.VMEM((outs, count, side, width), F32)] * fields,
        ),
        compiler_params=params(24),
        cost_estimate=cost(2 * size * side * group, size * 2 * (group + outs) + table.size * 2),
    )(where, *flat, scales, table, *after)


def scales_of(position, group, rows):
    distances = jnp.arange(group, dtype=jnp.int32)
    return (minus_one_to(position) * minus_one_to(position & distances)).astype(F32) / math.sqrt(rows * group)


def rotate_and_right(blocks, table, scales, lefts, position, plane):
    group = len(blocks)
    pieces = [len(block) for block in blocks]
    rows = blocks[0][0].shape[0]
    rank = lefts[0].shape[1]
    columns = blocks[-1][0].shape[1]
    _, count, side, _ = table.shape
    width = tile_width(columns)
    tiles = columns // width
    each = count // PLANE
    strip = side // count
    where = jnp.stack([position, plane >> 1])

    def body(where_ref, *refs):
        at, block_refs = 0, []
        for number in pieces:
            block_refs.append(refs[at : at + number])
            at += number
        scale_ref, table_ref = refs[at : at + 2]
        left_refs, out_refs = refs[at + 2 : at + 2 + group], refs[at + 2 + group : at + 2 + 2 * group]
        right_ref, even_ref, odd_ref, both_ref, total_ref = refs[-5:]
        step = pl.program_id(0)
        shown = jnp.maximum(step - 1, 0) * width

        def block_rows(d, number, first, size):
            if pieces[d] > 1:
                return block_refs[d][1 - number][pl.ds(first, size), :]
            pair = rows // 2
            start = pl.multiple_of((where_ref[1] ^ number) * pair + first, side)
            return block_refs[d][0][pl.ds(start, size), :]

        def mix(number, inside, field_ref):
            b = (where_ref[1] ^ number) * (count // 2) + inside
            first = pl.multiple_of(inside * side, side)
            products = [
                jnp.dot(both_ref[d, b], block_rows(d, number, first, side), preferred_element_type=F32)
                for d in range(group)
            ]
            total_ref[...] += sum([product[side:] for product in products[1:]], products[0][side:])
            for o, mixed in enumerate(butterflies([product[:side] for product in products])):
                field_ref[o, b] = mixed

        def spread(i, field_ref):
            for part in range(0, strip, 16):
                inner = pl.multiple_of(i * strip + part, 16)
                for o in range(group):
                    for start in range(0, width, 128):
                        lanes = slice(start, start + 128)
                        values = butterflies([field_ref[o, b, pl.ds(inner, 16), lanes] for b in range(count)])
                        if o == 0:
                            lanes = pl.ds(pl.multiple_of(shown + start, 128), 128)
                        for b in range(count):
                            turned = (values[b] * scale_ref[o]).astype(BF16)
                            out_refs[o][pl.ds(pl.multiple_of(b * side + inner, 16), 16), lanes] = turned

        def sweep(mixed_ref, spread_ref):
            for number in range(2):

                @pl.loop(0, count // 2, unroll=2)
                def _(inside, number=number):
                    if mixed_ref is not None:
                        mix(number, inside, mixed_ref)
                    if spread_ref is not None:
                        spread(number * (count // 2) + inside, spread_ref)

        @pl.when(step == 0)
        def _():
            for d in range(group):
                for b in range(count):
                    both_ref[d, b, :side, :] = table_ref[d, b]
                    both_ref[d, b, side:, :] = left_refs[d][b * side : (b + 1) * side, :].T

        @pl.when(step < tiles)
        def _():
            total_ref[...] = jnp.zeros_like(total_ref)

        fields = (even_ref, odd_ref)

        @pl.when(step == 0)
        def _():
            sweep(fields[0], None)

        for parity in range(2):

            @pl.when((step > 0) & (step < tiles) & (step % 2 == parity))
            def _(parity=parity):
                sweep(fields[parity], fields[1 - parity])

        @pl.when(step < tiles)
        def _():
            right_ref[...] = total_ref[...].astype(BF16)

        @pl.when(step == tiles)
        def _():
            sweep(None, fields[(tiles - 1) % 2])

    def place(piece):
        def index(j, where):
            j = jnp.minimum(j, tiles - 1)
            return 0, j if piece.shape[1] == columns else where[0] * tiles + j

        return pl.BlockSpec((piece.shape[0], width), index)

    flat = [piece for block in blocks for piece in block]
    field = pltpu.VMEM((group, count, side, width), F32)
    size = rows * columns
    return pl.pallas_call(
        body,
        out_shape=[pltpu.VMEM((rows, columns), BF16)]
        + [jax.ShapeDtypeStruct((rows, columns), BF16)] * (group - 1)
        + [jax.ShapeDtypeStruct((rank, columns), BF16)],
        grid_spec=pltpu.PrefetchScalarGridSpec(
            num_scalar_prefetch=1,
            grid=(tiles + 1,),
            in_specs=[place(piece) for piece in flat] + [SMEM, VMEM] + [VMEM] * group,
            out_specs=[VMEM]
            + [pl.BlockSpec((rows, width), lambda j, where: (0, jnp.maximum(j - 1, 0)))] * (group - 1)
            + [pl.BlockSpec((rank, width), lambda j, where: (0, jnp.minimum(j, tiles - 1)))],
            scratch_shapes=[
                field,
                field,
                pltpu.VMEM((group, count, side + rank, side), BF16),
                pltpu.VMEM((rank, width), F32),
            ],
        ),
        compiler_params=params(41),
        cost_estimate=cost(2 * size * (side + rank) * group, size * 2 * (2 * group - 1) + table.size * 2),
    )(where, *flat, scales, table, *lefts)


def project(accumulated, q_start, piece_at, position, group, out_types, after, copies=()):
    rows, columns = accumulated.shape
    rank = q_start.shape[1]
    share = columns // group
    piece = rows // PLANE
    tall = min(512, piece)
    steps = piece // tall

    def body(where_ref, a_ref, q_ref, *refs):
        out_refs = refs[len(after) + len(copies) :]
        product = jnp.dot(a_ref[...], q_ref[...], preferred_element_type=F32)
        for number, out_type in enumerate(out_types):

            @pl.when(pl.program_id(0) // steps == number)
            def _(number=number, out_type=out_type):
                out_refs[number][...] = product.astype(out_type)

        for d in range(1, group):
            lanes = pl.ds(pl.multiple_of((where_ref[1] ^ d) * share, 128), share)
            out_refs[len(out_types) + d - 1][...] = a_ref[:, lanes]

    def out_place(number):
        return pl.BlockSpec((tall, rank), lambda i, where: (jnp.clip(i - number * steps, 0, steps - 1), 0))

    def copy_row(i, where):
        return ((where[0] ^ (i // steps)) & 1) * steps + i % steps

    return pl.pallas_call(
        body,
        out_shape=[jax.ShapeDtypeStruct((piece, rank), out_type) for out_type in out_types]
        + [jax.ShapeDtypeStruct((2 * piece, share), BF16)] * (group - 1),
        grid_spec=pltpu.PrefetchScalarGridSpec(
            num_scalar_prefetch=1,
            grid=(len(out_types) * steps,),
            in_specs=[
                pl.BlockSpec((tall, columns), lambda i, where: ((where[0] ^ (i // steps)) * steps + i % steps, 0)),
                pl.BlockSpec((columns, rank), lambda i, where: (0, 0)),
            ]
            + [ANY] * (len(after) + len(copies)),
            out_specs=[out_place(number) for number in range(len(out_types))]
            + [pl.BlockSpec((tall, share), lambda i, where: (copy_row(i, where), 0))] * (group - 1),
        ),
        input_output_aliases={3 + len(after) + d: len(out_types) + d for d in range(len(copies))},
        compiler_params=params(24),
        cost_estimate=cost(2 * len(out_types) * piece * columns * rank, len(out_types) * piece * columns * 3),
    )(jnp.stack([piece_at, position]), accumulated, q_start, *after, *copies)


def split_sum(own, others, place, pieces, after):
    rows, rank = own.shape
    piece = rows // pieces

    def body(where_ref, own_ref, *refs):
        other_refs, out_refs = refs[: len(others)], refs[len(others) + len(after) :]
        for d in range(pieces):
            at = pl.ds(pl.multiple_of((where_ref[0] ^ d) * piece, piece), piece)
            total = own_ref[at, :]
            for ref in other_refs:
                total += ref[at, :].astype(F32)
            out_refs[d][...] = total.astype(out_refs[d].dtype)

    return pl.pallas_call(
        body,
        out_shape=[jax.ShapeDtypeStruct((piece, rank), F32 if d == 0 else BF16) for d in range(pieces)],
        in_specs=[pl.BlockSpec(memory_space=pltpu.SMEM)] + [pl.BlockSpec(memory_space=pltpu.VMEM)] * (1 + len(others)) + [ANY] * len(after),
        out_specs=[pl.BlockSpec(memory_space=pltpu.VMEM)] * pieces,
        compiler_params=params(24),
    )(place.reshape(1), own, *others, *after)


def assemble(parts, place, after=()):
    rows, rank = parts[0].shape
    count = len(parts)

    def body(where_ref, *refs):
        out_ref = refs[-1]
        for d in range(count):
            at = pl.ds(pl.multiple_of((where_ref[0] ^ d) * rows, rows), rows)
            out_ref[at, :] = refs[d][...]

    return pl.pallas_call(
        body,
        out_shape=jax.ShapeDtypeStruct((rows * count, rank), parts[0].dtype),
        in_specs=[pl.BlockSpec(memory_space=pltpu.SMEM)]
        + [pl.BlockSpec(memory_space=pltpu.VMEM)] * count
        + [ANY] * len(after),
        out_specs=pl.BlockSpec(memory_space=pltpu.VMEM),
        compiler_params=params(24),
    )(place.reshape(1), *parts, *after)


def right_piece(accumulated, left, piece_at, position, shares, earlier):
    rows, columns = accumulated.shape
    piece, rank = left.shape
    share = columns // shares
    width = 896 if share % 896 == 0 else tile_width(share)
    steps = columns // width
    each = steps // shares

    def body(where_ref, a_ref, left_ref, *refs):
        out_refs, gram_ref, turned_ref = refs[len(earlier) : -2], refs[-2], refs[-1]
        at = pl.program_id(0)

        @pl.when(at == 0)
        def _():
            turned_ref[...] = left_ref[...].T
            gram_ref[...] = jnp.dot(turned_ref[...], left_ref[...], preferred_element_type=F32)

        total = jnp.dot(turned_ref[...], a_ref[...], preferred_element_type=F32)
        if earlier:
            total += refs[0][...]
        for d in range(shares):

            @pl.when(at // each == where_ref[1] ^ d)
            def _(d=d):
                out_refs[d][...] = total

    def out_place(d):
        return pl.BlockSpec((rank, width), lambda j, where: (0, jnp.clip(j - (where[1] ^ d) * each, 0, each - 1)))

    whole = pl.BlockSpec((rank, width), lambda j, where: (0, j))
    return pl.pallas_call(
        body,
        out_shape=[jax.ShapeDtypeStruct((rank, share), F32)] * shares + [jax.ShapeDtypeStruct((rank, rank), F32)],
        grid_spec=pltpu.PrefetchScalarGridSpec(
            num_scalar_prefetch=1,
            grid=(steps,),
            in_specs=[
                pl.BlockSpec((piece, width), lambda j, where: (where[0], j)),
                pl.BlockSpec((piece, rank), lambda j, where: (0, 0)),
            ]
            + [whole] * len(earlier),
            out_specs=([out_place(d) for d in range(shares)] if shares > 1 else [whole])
            + [pl.BlockSpec((rank, rank), lambda j, where: (0, 0))],
            scratch_shapes=[pltpu.VMEM((rank, piece), BF16)],
        ),
        compiler_params=params(24),
        cost_estimate=cost(2 * piece * columns * rank, piece * columns * 2),
    )(jnp.stack([piece_at, position if shares > 1 else jnp.zeros_like(position)]), accumulated, left, *earlier)


def halves(value):
    high = value.astype(BF16)
    return high, (value - high.astype(F32)).astype(BF16)


def inverse_factor(gram):
    rank = gram.shape[0]
    lane = lax.broadcasted_iota(jnp.int32, (8, rank), 1)
    row = lax.broadcasted_iota(jnp.int32, (8, rank), 0)
    starts = range(0, rank, 8)
    left = [gram[start : start + 8, :] for start in starts]
    right = [jnp.where(lane == row + start, 1.0, 0.0).astype(F32) for start in starts]
    scales = []
    for home, start in enumerate(starts):

        def spread_columns(block):
            return [jnp.broadcast_to(left[block][:, start + i : start + i + 1], (8, rank)) for i in range(8)]

        columns, inverses = spread_columns(home), []
        scale = jnp.zeros((8, rank), F32)
        for i in range(8):
            root = lax.rsqrt(jnp.broadcast_to(columns[i][i : i + 1, :], (8, rank)))
            scale = jnp.where(row == i, root, scale)
            inverses.append(root * root)
            if i < 7:
                factor = jnp.where(row > i, columns[i] * inverses[i], 0.0)
                left[home] = left[home] - factor * left[home][i : i + 1, :]
                right[home] = right[home] - factor * right[home][i : i + 1, :]
                for after in range(i + 1, 8):
                    columns[after] = columns[after] - factor * columns[after][i : i + 1, :]
        scales.append(scale)
        for block in range(home + 1, len(left)):
            own = spread_columns(block)
            for i in range(8):
                factor = own[i] * inverses[i]
                left[block] = left[block] - factor * left[home][i : i + 1, :]
                right[block] = right[block] - factor * right[home][i : i + 1, :]
                for after in range(i + 1, 8):
                    own[after] = own[after] - factor * columns[after][i : i + 1, :]
    return jnp.concatenate([part * scale for part, scale in zip(right, scales)], axis=0)


def basis_of(blocks, table, scales):
    group = len(blocks)
    rows, rank = blocks[0].shape
    _, count, side, _ = table.shape

    def body(*refs):
        block_refs, scale_ref, table_ref = refs[:group], refs[group], refs[group + 1]
        inverse_ref, basis_ref, basis16_ref, field_ref, turned_ref = refs[group + 2 :]

        @pl.loop(0, count, unroll=4)
        def _(b):
            at = pl.ds(pl.multiple_of(b * side, side), side)
            mixed = jnp.dot(table_ref[0, b], block_refs[0][at, :], preferred_element_type=F32)
            for d in range(1, group):
                mixed += jnp.dot(table_ref[d, b], block_refs[d][at, :], preferred_element_type=F32)
            field_ref[b] = mixed

        @pl.loop(0, side // 16, unroll=2)
        def _(i):
            inner = pl.multiple_of(i * 16, 16)
            values = butterflies([field_ref[b, pl.ds(inner, 16), :] for b in range(count)])
            for b in range(count):
                turned_ref[pl.ds(pl.multiple_of(b * side + inner, 16), 16), :] = values[b] * scale_ref[0]

        grams = [jnp.dot(ref[...].T, ref[...], preferred_element_type=F32) for ref in block_refs]
        while len(grams) > 1:
            grams = [low + high for low, high in zip(grams[::2], grams[1::2])]
        inverse = inverse_factor(grams[0])
        inverse_ref[...] = inverse
        high, low = halves(inverse.T)
        turned_high, turned_low = halves(turned_ref[...])
        both = jnp.concatenate([turned_high, turned_low], axis=1)
        basis = jnp.dot(both, jnp.concatenate([high, high], axis=0), preferred_element_type=F32)
        basis += jnp.dot(turned_high, low, preferred_element_type=F32)
        basis_ref[...] = basis
        basis16_ref[...] = basis.astype(BF16)

    return pl.pallas_call(
        body,
        out_shape=[
            jax.ShapeDtypeStruct((rank, rank), F32),
            jax.ShapeDtypeStruct((rows, rank), F32),
            jax.ShapeDtypeStruct((rows, rank), BF16),
        ],
        in_specs=[VMEM] * group + [SMEM, VMEM],
        out_specs=[VMEM] * 3,
        scratch_shapes=[pltpu.VMEM((count, side, rank), F32), pltpu.VMEM((rows, rank), F32)],
        compiler_params=params(10),
        cost_estimate=cost(8 * 10**9, 60 * 10**6),
    )(*blocks, scales, table)


def residual(rotated, basis16, right, columns, owner, resident, into=()):
    rows, share = rotated.shape
    rank = right.shape[0]
    tall = min(512, rows)

    def body(where_ref, rotated_ref, basis_ref, right_ref, *refs):
        out_ref, factor_ref, right16_ref = refs[len(into) :]

        @pl.when(pl.program_id(0) == 0)
        def _():
            right16_ref[...] = right_ref[...].astype(BF16)
            factor_ref[...] = right_ref[...].T

        part = pl.ds(pl.multiple_of(pl.program_id(0) * tall, tall), tall) if resident else slice(None)
        for start in range(0, share, 256):
            lanes = slice(start, min(start + 256, share))
            approx = jnp.dot(basis_ref[...], right16_ref[:, lanes], preferred_element_type=F32)
            out_ref[:, lanes] = (rotated_ref[part, lanes].astype(F32) - approx).astype(out_ref.dtype)

    return pl.pallas_call(
        body,
        out_shape=[jax.ShapeDtypeStruct((rows, columns), BF16), jax.ShapeDtypeStruct((columns, rank), F32)],
        grid_spec=pltpu.PrefetchScalarGridSpec(
            num_scalar_prefetch=1,
            grid=(rows // tall,),
            in_specs=[
                VMEM if resident else pl.BlockSpec((tall, share), lambda i, where: (i, 0)),
                pl.BlockSpec((tall, rank), lambda i, where: (i, 0)),
                pl.BlockSpec((rank, share), lambda i, where: (0, 0)),
            ]
            + [ANY] * len(into),
            out_specs=[
                pl.BlockSpec((tall, share), lambda i, where: (i, where[0])),
                pl.BlockSpec((share, rank), lambda i, where: (where[0], 0)),
            ],
            scratch_shapes=[pltpu.VMEM((rank, share), BF16)],
        ),
        input_output_aliases={4: 0, 5: 1} if into else {},
        compiler_params=params(10),
        cost_estimate=cost(2 * rows * share * rank, rows * share * 2),
    )(owner.reshape(1), rotated, basis16, right, *into)


def from_distance(block, axis, distance):
    count = lax.axis_size(axis)
    return lax.ppermute(block, axis, [(p, p ^ distance) for p in range(count)])


def from_plane(block, distance):
    count, mp_count = REPLICAS * lax.axis_size("mp"), lax.axis_size("mp")
    change = (distance & 1) | (distance >> 1) * mp_count
    return lax.ppermute(block, ("rep", "mp"), [(p, p ^ change) for p in range(count)])


def from_line(block, distance):
    return from_distance(block, "mp", distance << 1)


def local(accumulated, signs, q_start):
    rows, columns = accumulated.shape
    rank = q_start.shape[1]
    group = lax.axis_size("pos")
    position = lax.axis_index("pos")
    mp_index = lax.axis_index("mp")
    plane = lax.axis_index("rep") * 2 + (mp_index & 1)
    line, lines = mp_index >> 1, lax.axis_size("mp") // 2
    share = columns // group
    shared = share % 128 == 0 and rows % (256 * PLANE) == 0
    others = range(1, group)

    came, after, copies = [], (), ()
    other_pieces = [[] for _ in others]
    for sent in ((3,), (2,), (1,), (0,)):
        out_types = [BF16 if d else F32 for d in sent]
        results = project(
            accumulated, q_start, plane ^ sent[0], position, group if shared else 1, out_types, after, copies
        )
        parts, copies = results[: len(sent)], tuple(results[len(sent) :])
        after = (parts[-1],)
        came += [from_plane(part, d) for part, d in zip(parts, sent) if d]
        if sent[0] == 1:
            after += (came[0],)
        if sent[0] % 2 == 0:
            for e, copy in enumerate(copies):
                other_pieces[e].append(from_distance(copy, "pos", e + 1))
            copies = ()
    table = signed_hadamard(signs, position, group, rows)
    scales = scales_of(position, group, rows)
    if not shared:
        other_pieces = [[from_distance(accumulated, "pos", d)] for d in others]
    blocks = [[accumulated]] + other_pieces

    own, *sent = split_sum(parts[0], came, line, lines, (table, scales))
    came = [from_line(sent[d - 1], d) for d in range(1, lines)]
    mine16 = sum([part.astype(F32) for part in came], own).astype(BF16)
    near16 = assemble([mine16] + [from_line(mine16, d) for d in range(1, lines)], line)
    far16 = [near16] + [from_plane(near16, d) for d in range(1, PLANE)]
    own16 = assemble(far16, plane)
    around16 = [own16] + [from_distance(own16, "pos", d) for d in others]

    if shared:
        *rotated, half = rotate_and_right(blocks, table, scales, around16, position, plane)
        rotated = rotated[:1] + [from_distance(part, "pos", d + 1) for d, part in enumerate(rotated[1:])]
        half = half.astype(F32) + from_distance(half, "rep", 1).astype(F32)
    else:
        rotated = rotate(blocks, table, position, plane, BF16, 1)
        totals = []
        for d in range(PLANE):
            *totals, _ = right_piece(accumulated, far16[d], plane ^ d, position, 1, totals)
        half = lax.psum(totals[0], ("rep", "pos"))
    inverse, p_basis, basis16 = basis_of(around16, table, scales)

    right = jnp.dot(inverse, half, precision=lax.Precision.HIGHEST) / REPLICAS
    if not shared:
        new_error, q_factor = residual(rotated[0], basis16, right, columns, jnp.zeros((), jnp.int32), False)
        return (new_error, p_basis, q_factor)
    rights = [right] + [from_distance(right, "pos", d) for d in others]
    results = ()
    for d in range(group):
        results = residual(rotated[d], basis16, rights[d], columns, position ^ d, d == 0, results)
    new_error, q_factor = results
    return (new_error, p_basis, q_factor)


def solution(mesh):
    dp_count, mp_count = mesh.shape["dp"], mesh.shape["mp"]
    fine = Mesh(
        mesh.devices.reshape(REPLICAS, dp_count // REPLICAS, mp_count), ("rep", "pos", "mp")
    )
    rows_of = ("rep", "pos")
    in_specs = (P(rows_of, "mp"), P(), P("mp", None))
    out_specs = (P(rows_of, "mp"), P(rows_of, None), P("mp", None))
    return jax.shard_map(local, mesh=fine, in_specs=in_specs, out_specs=out_specs, check_vma=False)
```

```python
import functools
import math

import jax
import jax.numpy as jnp
from jax import lax
from jax.experimental import pallas as pl
from jax.experimental.pallas import tpu as pltpu
from jax.sharding import Mesh, PartitionSpec as P

REPLICAS = 2
PLANE = 2 * REPLICAS
F32 = jnp.float32
BF16 = jnp.bfloat16
ANY = pl.BlockSpec(memory_space=pl.ANY)
VMEM = pl.BlockSpec(memory_space=pltpu.VMEM)
SMEM = pl.BlockSpec(memory_space=pltpu.SMEM)
MIB = 1024 * 1024


def cost(flops, size):
    return pl.CostEstimate(flops=flops, bytes_accessed=size, transcendentals=0)


def params(mib):
    return pltpu.CompilerParams(vmem_limit_bytes=mib * MIB)


def sylvester(size):
    index = jnp.arange(size, dtype=jnp.int32)
    parity = lax.population_count(index[:, None] & index[None, :]) & 1
    return (1 - 2 * parity).astype(F32)


def butterflies(values):
    values = list(values)
    step = 1
    while step < len(values):
        for low in range(len(values)):
            if not low & step:
                high = low | step
                values[low], values[high] = values[low] + values[high], values[low] - values[high]
        step *= 2
    return values


def tile_width(columns):
    return 256 if columns % 256 == 0 else 128


def minus_one_to(number):
    return 1 - 2 * (lax.population_count(number) & 1)


def signed_hadamard(signs, position, group, rows):
    side = min(256, rows)
    parts = []
    for distance in range(group):
        mine = lax.dynamic_slice_in_dim(signs, (position ^ distance) * rows, rows)
        parts.append((2 * mine - 1) * minus_one_to(position & distance))
    flips = jnp.stack(parts).astype(F32).reshape(group, rows // side, 1, side)
    return (sylvester(side) * flips).astype(BF16)


def rotate_body(group, outs, pieces, *refs):
    where_ref, refs = refs[0], refs[1:]
    total = sum(pieces)
    block_refs, at = [], 0
    for number in pieces:
        block_refs.append(refs[at : at + number])
        at += number
    scale_ref, table_ref = refs[total], refs[total + 1]
    fields = 2 if pl.num_programs(0) > 1 else 1
    out_refs, field_refs = refs[-fields - outs : -fields], refs[-fields:]
    _, count, side, width = field_refs[0].shape
    cuts = PLANE if max(pieces) > 1 else 1
    each = count // cuts
    strip = side // count

    def mix(e, inside, field_ref):
        b = (where_ref[1] ^ e) * each + inside
        parts = []
        for d in range(group):
            if pieces[d] > 1:
                array, part = divmod(PLANE - 1 - e, PLANE // pieces[d])
                ref, first = block_refs[d][array], (part * each + inside) * side
            else:
                ref, first = block_refs[d][0], b * side
            rows = pl.ds(pl.multiple_of(first, side), side)
            parts.append(jnp.dot(table_ref[d, b], ref[rows, :], preferred_element_type=F32))
        mixed = butterflies(parts) if outs > 1 else [sum(parts[1:], parts[0])]
        for o in range(outs):
            field_ref[o, b] = mixed[o]

    def spread(i, field_ref):
        for part in range(0, strip, 16):
            inner = pl.multiple_of(i * strip + part, 16)
            for o in range(outs):
                for start in range(0, width, 128):
                    lanes = slice(start, start + 128)
                    values = butterflies([field_ref[o, b, pl.ds(inner, 16), lanes] for b in range(count)])
                    for b in range(count):
                        turned = (values[b] * scale_ref[o]).astype(out_refs[o].dtype)
                        out_refs[o][pl.ds(pl.multiple_of(b * side + inner, 16), 16), lanes] = turned

    def sweep(mixed_ref, spread_ref):
        for e in range(cuts):

            @pl.loop(0, each, unroll=2)
            def _(inside, e=e):
                if mixed_ref is not None:
                    mix(e, inside, mixed_ref)
                if spread_ref is not None:
                    spread(e * each + inside, spread_ref)

    if fields == 1:
        sweep(field_refs[0], None)
        sweep(None, field_refs[0])
        return
    odd = pl.program_id(0) % 2 == 1

    @pl.when(jnp.logical_not(odd))
    def _():
        sweep(field_refs[0], field_refs[1])

    @pl.when(odd)
    def _():
        sweep(field_refs[1], field_refs[0])


def rotate(blocks, table, position, plane, out_type, outs, first=0, steps=None, after=()):
    group = len(blocks)
    pieces = [len(block) for block in blocks]
    rows = sum(piece.shape[0] for piece in blocks[0])
    columns = blocks[-1][0].shape[1]
    _, count, side, _ = table.shape
    width = tile_width(columns)
    tiles = columns // width
    steps = tiles if steps is None else steps
    distances = jnp.arange(group, dtype=jnp.int32)
    scales = (minus_one_to(position) * minus_one_to(position & distances)).astype(F32) / math.sqrt(rows * group)
    where = jnp.stack([position, plane if max(pieces) > 1 else jnp.zeros_like(plane)])

    fields = 2 if steps > 1 else 1

    def place(piece):
        def index(j, where):
            j = first + jnp.minimum(j, steps - 1)
            return 0, j if piece.shape[1] == columns else where[0] * tiles + j

        return pl.BlockSpec((piece.shape[0], width), index)

    flat = [piece for block in blocks for piece in block]
    kept = 1 + len(flat) + 2

    def body(*refs):
        rotate_body(group, outs, pieces, *refs[:kept], *refs[kept + len(after) :])

    size = rows * steps * width
    return pl.pallas_call(
        body,
        out_shape=[jax.ShapeDtypeStruct((rows, steps * width), out_type)] * outs,
        grid_spec=pltpu.PrefetchScalarGridSpec(
            num_scalar_prefetch=1,
            grid=(steps + fields - 1,),
            in_specs=[place(piece) for piece in flat]
            + [pl.BlockSpec(memory_space=pltpu.SMEM), pl.BlockSpec(table.shape, lambda j, where: (0, 0, 0, 0))]
            + [ANY] * len(after),
            out_specs=[pl.BlockSpec((rows, width), lambda j, where: (0, jnp.maximum(j - (fields - 1), 0)))] * outs,
            scratch_shapes=[pltpu.VMEM((outs, count, side, width), F32)] * fields,
        ),
        compiler_params=params(24),
        cost_estimate=cost(2 * size * side * group, size * 2 * (group + outs) + table.size * 2),
    )(where, *flat, scales, table, *after)


def scales_of(position, group, rows):
    distances = jnp.arange(group, dtype=jnp.int32)
    return (minus_one_to(position) * minus_one_to(position & distances)).astype(F32) / math.sqrt(rows * group)


def rotate_and_right(blocks, table, scales, lefts, position, plane):
    group = len(blocks)
    pieces = [len(block) for block in blocks]
    rows = blocks[0][0].shape[0]
    rank = lefts[0].shape[1]
    columns = blocks[-1][0].shape[1]
    _, count, side, _ = table.shape
    width = tile_width(columns)
    tiles = columns // width
    each = count // PLANE
    strip = side // count
    where = jnp.stack([position, plane >> 1])

    def body(where_ref, *refs):
        at, block_refs = 0, []
        for number in pieces:
            block_refs.append(refs[at : at + number])
            at += number
        scale_ref, table_ref = refs[at : at + 2]
        left_refs, out_refs = refs[at + 2 : at + 2 + group], refs[at + 2 + group : at + 2 + 2 * group]
        right_ref, even_ref, odd_ref, both_ref, total_ref = refs[-5:]
        step = pl.program_id(0)
        shown = jnp.maximum(step - 1, 0) * width

        def block_rows(d, number, first, size):
            if pieces[d] > 1:
                return block_refs[d][1 - number][pl.ds(first, size), :]
            pair = rows // 2
            start = pl.multiple_of((where_ref[1] ^ number) * pair + first, side)
            return block_refs[d][0][pl.ds(start, size), :]

        def mix(number, inside, field_ref):
            b = (where_ref[1] ^ number) * (count // 2) + inside
            first = pl.multiple_of(inside * side, side)
            products = [
                jnp.dot(both_ref[d, b], block_rows(d, number, first, side), preferred_element_type=F32)
                for d in range(group)
            ]
            total_ref[...] += sum([product[side:] for product in products[1:]], products[0][side:])
            for o, mixed in enumerate(butterflies([product[:side] for product in products])):
                field_ref[o, b] = mixed

        def spread(i, field_ref):
            for part in range(0, strip, 16):
                inner = pl.multiple_of(i * strip + part, 16)
                for o in range(group):
                    for start in range(0, width, 128):
                        lanes = slice(start, start + 128)
                        values = butterflies([field_ref[o, b, pl.ds(inner, 16), lanes] for b in range(count)])
                        if o == 0:
                            lanes = pl.ds(pl.multiple_of(shown + start, 128), 128)
                        for b in range(count):
                            turned = (values[b] * scale_ref[o]).astype(BF16)
                            out_refs[o][pl.ds(pl.multiple_of(b * side + inner, 16), 16), lanes] = turned

        def sweep(mixed_ref, spread_ref):
            for number in range(2):

                @pl.loop(0, count // 2, unroll=2)
                def _(inside, number=number):
                    if mixed_ref is not None:
                        mix(number, inside, mixed_ref)
                    if spread_ref is not None:
                        spread(number * (count // 2) + inside, spread_ref)

        @pl.when(step == 0)
        def _():
            for d in range(group):
                for b in range(count):
                    both_ref[d, b, :side, :] = table_ref[d, b]
                    both_ref[d, b, side:, :] = left_refs[d][b * side : (b + 1) * side, :].T

        @pl.when(step < tiles)
        def _():
            total_ref[...] = jnp.zeros_like(total_ref)

        fields = (even_ref, odd_ref)

        @pl.when(step == 0)
        def _():
            sweep(fields[0], None)

        for parity in range(2):

            @pl.when((step > 0) & (step < tiles) & (step % 2 == parity))
            def _(parity=parity):
                sweep(fields[parity], fields[1 - parity])

        @pl.when(step < tiles)
        def _():
            right_ref[...] = total_ref[...].astype(BF16)

        @pl.when(step == tiles)
        def _():
            sweep(None, fields[(tiles - 1) % 2])

    def place(piece):
        def index(j, where):
            j = jnp.minimum(j, tiles - 1)
            return 0, j if piece.shape[1] == columns else where[0] * tiles + j

        return pl.BlockSpec((piece.shape[0], width), index)

    flat = [piece for block in blocks for piece in block]
    field = pltpu.VMEM((group, count, side, width), F32)
    size = rows * columns
    return pl.pallas_call(
        body,
        out_shape=[pltpu.VMEM((rows, columns), BF16)]
        + [jax.ShapeDtypeStruct((rows, columns), BF16)] * (group - 1)
        + [jax.ShapeDtypeStruct((rank, columns), BF16)],
        grid_spec=pltpu.PrefetchScalarGridSpec(
            num_scalar_prefetch=1,
            grid=(tiles + 1,),
            in_specs=[place(piece) for piece in flat] + [SMEM, VMEM] + [VMEM] * group,
            out_specs=[VMEM]
            + [pl.BlockSpec((rows, width), lambda j, where: (0, jnp.maximum(j - 1, 0)))] * (group - 1)
            + [pl.BlockSpec((rank, width), lambda j, where: (0, jnp.minimum(j, tiles - 1)))],
            scratch_shapes=[
                field,
                field,
                pltpu.VMEM((group, count, side + rank, side), BF16),
                pltpu.VMEM((rank, width), F32),
            ],
        ),
        compiler_params=params(41),
        cost_estimate=cost(2 * size * (side + rank) * group, size * 2 * (2 * group - 1) + table.size * 2),
    )(where, *flat, scales, table, *lefts)


def project(accumulated, q_start, piece_at, position, group, out_types, after, copies=()):
    rows, columns = accumulated.shape
    rank = q_start.shape[1]
    share = columns // group
    piece = rows // PLANE
    tall = min(512, piece)
    steps = piece // tall

    def body(where_ref, a_ref, q_ref, *refs):
        out_refs = refs[len(after) + len(copies) :]
        product = jnp.dot(a_ref[...], q_ref[...], preferred_element_type=F32)
        for number, out_type in enumerate(out_types):

            @pl.when(pl.program_id(0) // steps == number)
            def _(number=number, out_type=out_type):
                out_refs[number][...] = product.astype(out_type)

        for d in range(1, group):
            lanes = pl.ds(pl.multiple_of((where_ref[1] ^ d) * share, 128), share)
            out_refs[len(out_types) + d - 1][...] = a_ref[:, lanes]

    def out_place(number):
        return pl.BlockSpec((tall, rank), lambda i, where: (jnp.clip(i - number * steps, 0, steps - 1), 0))

    def copy_row(i, where):
        return ((where[0] ^ (i // steps)) & 1) * steps + i % steps

    return pl.pallas_call(
        body,
        out_shape=[jax.ShapeDtypeStruct((piece, rank), out_type) for out_type in out_types]
        + [jax.ShapeDtypeStruct((2 * piece, share), BF16)] * (group - 1),
        grid_spec=pltpu.PrefetchScalarGridSpec(
            num_scalar_prefetch=1,
            grid=(len(out_types) * steps,),
            in_specs=[
                pl.BlockSpec((tall, columns), lambda i, where: ((where[0] ^ (i // steps)) * steps + i % steps, 0)),
                pl.BlockSpec((columns, rank), lambda i, where: (0, 0)),
            ]
            + [ANY] * (len(after) + len(copies)),
            out_specs=[out_place(number) for number in range(len(out_types))]
            + [pl.BlockSpec((tall, share), lambda i, where: (copy_row(i, where), 0))] * (group - 1),
        ),
        input_output_aliases={3 + len(after) + d: len(out_types) + d for d in range(len(copies))},
        compiler_params=params(24),
        cost_estimate=cost(2 * len(out_types) * piece * columns * rank, len(out_types) * piece * columns * 3),
    )(jnp.stack([piece_at, position]), accumulated, q_start, *after, *copies)


def split_sum(own, others, place, pieces, after):
    rows, rank = own.shape
    piece = rows // pieces

    def body(where_ref, own_ref, *refs):
        other_refs, out_refs = refs[: len(others)], refs[len(others) + len(after) :]
        for d in range(pieces):
            at = pl.ds(pl.multiple_of((where_ref[0] ^ d) * piece, piece), piece)
            total = own_ref[at, :]
            for ref in other_refs:
                total += ref[at, :].astype(F32)
            out_refs[d][...] = total.astype(out_refs[d].dtype)

    return pl.pallas_call(
        body,
        out_shape=[jax.ShapeDtypeStruct((piece, rank), F32 if d == 0 else BF16) for d in range(pieces)],
        in_specs=[pl.BlockSpec(memory_space=pltpu.SMEM)] + [pl.BlockSpec(memory_space=pltpu.VMEM)] * (1 + len(others) + len(after)),
        out_specs=[pl.BlockSpec(memory_space=pltpu.VMEM)] * pieces,
        compiler_params=params(24),
    )(place.reshape(1), own, *others, *after)


def assemble(parts, place, after=()):
    rows, rank = parts[0].shape
    count = len(parts)

    def body(where_ref, *refs):
        out_ref = refs[-1]
        for d in range(count):
            at = pl.ds(pl.multiple_of((where_ref[0] ^ d) * rows, rows), rows)
            out_ref[at, :] = refs[d][...]

    return pl.pallas_call(
        body,
        out_shape=jax.ShapeDtypeStruct((rows * count, rank), parts[0].dtype),
        in_specs=[pl.BlockSpec(memory_space=pltpu.SMEM)]
        + [pl.BlockSpec(memory_space=pltpu.VMEM)] * count
        + [ANY] * len(after),
        out_specs=pl.BlockSpec(memory_space=pltpu.VMEM),
        compiler_params=params(24),
    )(place.reshape(1), *parts, *after)


def right_piece(accumulated, left, piece_at, position, shares, earlier):
    rows, columns = accumulated.shape
    piece, rank = left.shape
    share = columns // shares
    width = 896 if share % 896 == 0 else tile_width(share)
    steps = columns // width
    each = steps // shares

    def body(where_ref, a_ref, left_ref, *refs):
        out_refs, gram_ref, turned_ref = refs[len(earlier) : -2], refs[-2], refs[-1]
        at = pl.program_id(0)

        @pl.when(at == 0)
        def _():
            turned_ref[...] = left_ref[...].T
            gram_ref[...] = jnp.dot(turned_ref[...], left_ref[...], preferred_element_type=F32)

        total = jnp.dot(turned_ref[...], a_ref[...], preferred_element_type=F32)
        if earlier:
            total += refs[0][...]
        for d in range(shares):

            @pl.when(at // each == where_ref[1] ^ d)
            def _(d=d):
                out_refs[d][...] = total

    def out_place(d):
        return pl.BlockSpec((rank, width), lambda j, where: (0, jnp.clip(j - (where[1] ^ d) * each, 0, each - 1)))

    whole = pl.BlockSpec((rank, width), lambda j, where: (0, j))
    return pl.pallas_call(
        body,
        out_shape=[jax.ShapeDtypeStruct((rank, share), F32)] * shares + [jax.ShapeDtypeStruct((rank, rank), F32)],
        grid_spec=pltpu.PrefetchScalarGridSpec(
            num_scalar_prefetch=1,
            grid=(steps,),
            in_specs=[
                pl.BlockSpec((piece, width), lambda j, where: (where[0], j)),
                pl.BlockSpec((piece, rank), lambda j, where: (0, 0)),
            ]
            + [whole] * len(earlier),
            out_specs=([out_place(d) for d in range(shares)] if shares > 1 else [whole])
            + [pl.BlockSpec((rank, rank), lambda j, where: (0, 0))],
            scratch_shapes=[pltpu.VMEM((rank, piece), BF16)],
        ),
        compiler_params=params(24),
        cost_estimate=cost(2 * piece * columns * rank, piece * columns * 2),
    )(jnp.stack([piece_at, position if shares > 1 else jnp.zeros_like(position)]), accumulated, left, *earlier)


def halves(value):
    high = value.astype(BF16)
    return high, (value - high.astype(F32)).astype(BF16)


def inverse_factor(gram):
    rank = gram.shape[0]
    lane = lax.broadcasted_iota(jnp.int32, (8, rank), 1)
    row = lax.broadcasted_iota(jnp.int32, (8, rank), 0)
    starts = range(0, rank, 8)
    left = [gram[start : start + 8, :] for start in starts]
    right = [jnp.where(lane == row + start, 1.0, 0.0).astype(F32) for start in starts]
    scales = []
    for home, start in enumerate(starts):

        def spread_columns(block):
            return [jnp.broadcast_to(left[block][:, start + i : start + i + 1], (8, rank)) for i in range(8)]

        columns, inverses = spread_columns(home), []
        scale = jnp.zeros((8, rank), F32)
        for i in range(8):
            root = lax.rsqrt(jnp.broadcast_to(columns[i][i : i + 1, :], (8, rank)))
            scale = jnp.where(row == i, root, scale)
            inverses.append(root * root)
            if i < 7:
                factor = jnp.where(row > i, columns[i] * inverses[i], 0.0)
                left[home] = left[home] - factor * left[home][i : i + 1, :]
                right[home] = right[home] - factor * right[home][i : i + 1, :]
                for after in range(i + 1, 8):
                    columns[after] = columns[after] - factor * columns[after][i : i + 1, :]
        scales.append(scale)
        for block in range(home + 1, len(left)):
            own = spread_columns(block)
            for i in range(8):
                factor = own[i] * inverses[i]
                left[block] = left[block] - factor * left[home][i : i + 1, :]
                right[block] = right[block] - factor * right[home][i : i + 1, :]
                for after in range(i + 1, 8):
                    own[after] = own[after] - factor * columns[after][i : i + 1, :]
    return jnp.concatenate([part * scale for part, scale in zip(right, scales)], axis=0)


def basis_of(blocks, table, scales):
    group = len(blocks)
    rows, rank = blocks[0].shape
    _, count, side, _ = table.shape

    def body(*refs):
        block_refs, scale_ref, table_ref = refs[:group], refs[group], refs[group + 1]
        inverse_ref, basis_ref, basis16_ref, field_ref, turned_ref = refs[group + 2 :]

        @pl.loop(0, count, unroll=4)
        def _(b):
            at = pl.ds(pl.multiple_of(b * side, side), side)
            mixed = jnp.dot(table_ref[0, b], block_refs[0][at, :], preferred_element_type=F32)
            for d in range(1, group):
                mixed += jnp.dot(table_ref[d, b], block_refs[d][at, :], preferred_element_type=F32)
            field_ref[b] = mixed

        @pl.loop(0, side // 16, unroll=2)
        def _(i):
            inner = pl.multiple_of(i * 16, 16)
            values = butterflies([field_ref[b, pl.ds(inner, 16), :] for b in range(count)])
            for b in range(count):
                turned_ref[pl.ds(pl.multiple_of(b * side + inner, 16), 16), :] = values[b] * scale_ref[0]

        grams = [jnp.dot(ref[...].T, ref[...], preferred_element_type=F32) for ref in block_refs]
        while len(grams) > 1:
            grams = [low + high for low, high in zip(grams[::2], grams[1::2])]
        inverse = inverse_factor(grams[0])
        inverse_ref[...] = inverse
        high, low = halves(inverse.T)
        turned_high, turned_low = halves(turned_ref[...])
        both = jnp.concatenate([turned_high, turned_low], axis=1)
        basis = jnp.dot(both, jnp.concatenate([high, high], axis=0), preferred_element_type=F32)
        basis += jnp.dot(turned_high, low, preferred_element_type=F32)
        basis_ref[...] = basis
        basis16_ref[...] = basis.astype(BF16)

    return pl.pallas_call(
        body,
        out_shape=[
            jax.ShapeDtypeStruct((rank, rank), F32),
            jax.ShapeDtypeStruct((rows, rank), F32),
            jax.ShapeDtypeStruct((rows, rank), BF16),
        ],
        in_specs=[VMEM] * group + [SMEM, VMEM],
        out_specs=[VMEM] * 3,
        scratch_shapes=[pltpu.VMEM((count, side, rank), F32), pltpu.VMEM((rows, rank), F32)],
        compiler_params=params(10),
        cost_estimate=cost(8 * 10**9, 60 * 10**6),
    )(*blocks, scales, table)


def residual(rotated, basis16, right, columns, owner, resident, into=()):
    rows, share = rotated.shape
    rank = right.shape[0]
    tall = min(512, rows)

    def body(where_ref, rotated_ref, basis_ref, right_ref, *refs):
        out_ref, factor_ref, right16_ref = refs[len(into) :]

        @pl.when(pl.program_id(0) == 0)
        def _():
            right16_ref[...] = right_ref[...].astype(BF16)
            factor_ref[...] = right_ref[...].T

        part = pl.ds(pl.multiple_of(pl.program_id(0) * tall, tall), tall) if resident else slice(None)
        for start in range(0, share, 256):
            lanes = slice(start, min(start + 256, share))
            approx = jnp.dot(basis_ref[...], right16_ref[:, lanes], preferred_element_type=F32)
            out_ref[:, lanes] = (rotated_ref[part, lanes].astype(F32) - approx).astype(out_ref.dtype)

    return pl.pallas_call(
        body,
        out_shape=[jax.ShapeDtypeStruct((rows, columns), BF16), jax.ShapeDtypeStruct((columns, rank), F32)],
        grid_spec=pltpu.PrefetchScalarGridSpec(
            num_scalar_prefetch=1,
            grid=(rows // tall,),
            in_specs=[
                VMEM if resident else pl.BlockSpec((tall, share), lambda i, where: (i, 0)),
                pl.BlockSpec((tall, rank), lambda i, where: (i, 0)),
                pl.BlockSpec((rank, share), lambda i, where: (0, 0)),
            ]
            + [ANY] * len(into),
            out_specs=[
                pl.BlockSpec((tall, share), lambda i, where: (i, where[0])),
                pl.BlockSpec((share, rank), lambda i, where: (where[0], 0)),
            ],
            scratch_shapes=[pltpu.VMEM((rank, share), BF16)],
        ),
        input_output_aliases={4: 0, 5: 1} if into else {},
        compiler_params=params(10),
        cost_estimate=cost(2 * rows * share * rank, rows * share * 2),
    )(owner.reshape(1), rotated, basis16, right, *into)


def from_distance(block, axis, distance):
    count = lax.axis_size(axis)
    return lax.ppermute(block, axis, [(p, p ^ distance) for p in range(count)])


def from_plane(block, distance):
    count, mp_count = REPLICAS * lax.axis_size("mp"), lax.axis_size("mp")
    change = (distance & 1) | (distance >> 1) * mp_count
    return lax.ppermute(block, ("rep", "mp"), [(p, p ^ change) for p in range(count)])


def from_line(block, distance):
    return from_distance(block, "mp", distance << 1)


def local(accumulated, signs, q_start):
    rows, columns = accumulated.shape
    rank = q_start.shape[1]
    group = lax.axis_size("pos")
    position = lax.axis_index("pos")
    mp_index = lax.axis_index("mp")
    plane = lax.axis_index("rep") * 2 + (mp_index & 1)
    line, lines = mp_index >> 1, lax.axis_size("mp") // 2
    share = columns // group
    shared = share % 128 == 0 and rows % (256 * PLANE) == 0
    others = range(1, group)

    came, after, copies = [], (), ()
    other_pieces = [[] for _ in others]
    for sent in ((3,), (2,), (1,), (0,)):
        out_types = [BF16 if d else F32 for d in sent]
        results = project(
            accumulated, q_start, plane ^ sent[0], position, group if shared else 1, out_types, after, copies
        )
        parts, copies = results[: len(sent)], tuple(results[len(sent) :])
        after = (parts[-1],)
        came += [from_plane(part, d) for part, d in zip(parts, sent) if d]
        if sent[0] == 1:
            after += (came[0],)
        if sent[0] % 2 == 0:
            for e, copy in enumerate(copies):
                other_pieces[e].append(from_distance(copy, "pos", e + 1))
            copies = ()
    table = signed_hadamard(signs, position, group, rows)
    scales = scales_of(position, group, rows)
    if not shared:
        other_pieces = [[from_distance(accumulated, "pos", d)] for d in others]
    blocks = [[accumulated]] + other_pieces

    own, *sent = split_sum(parts[0], came, line, lines, (table,))
    came = [from_line(sent[d - 1], d) for d in range(1, lines)]
    mine16 = sum([part.astype(F32) for part in came], own).astype(BF16)
    near16 = assemble([mine16] + [from_line(mine16, d) for d in range(1, lines)], line)
    far16 = [near16] + [from_plane(near16, d) for d in range(1, PLANE)]
    own16 = assemble(far16, plane)
    around16 = [own16] + [from_distance(own16, "pos", d) for d in others]

    if shared:
        *rotated, half = rotate_and_right(blocks, table, scales, around16, position, plane)
        rotated = rotated[:1] + [from_distance(part, "pos", d + 1) for d, part in enumerate(rotated[1:])]
        half = half.astype(F32) + from_distance(half, "rep", 1).astype(F32)
    else:
        rotated = rotate(blocks, table, position, plane, BF16, 1)
        totals = []
        for d in range(PLANE):
            *totals, _ = right_piece(accumulated, far16[d], plane ^ d, position, 1, totals)
        half = lax.psum(totals[0], ("rep", "pos"))
    inverse, p_basis, basis16 = basis_of(around16, table, scales)

    right = jnp.dot(inverse, half, precision=lax.Precision.HIGHEST) / REPLICAS
    if not shared:
        new_error, q_factor = residual(rotated[0], basis16, right, columns, jnp.zeros((), jnp.int32), False)
        return (new_error, p_basis, q_factor)
    rights = [right] + [from_distance(right, "pos", d) for d in others]
    results = ()
    for d in range(group):
        results = residual(rotated[d], basis16, rights[d], columns, position ^ d, d == 0, results)
    new_error, q_factor = results
    return (new_error, p_basis, q_factor)


def solution(mesh):
    dp_count, mp_count = mesh.shape["dp"], mesh.shape["mp"]
    fine = Mesh(
        mesh.devices.reshape(REPLICAS, dp_count // REPLICAS, mp_count), ("rep", "pos", "mp")
    )
    rows_of = ("rep", "pos")
    in_specs = (P(rows_of, "mp"), P(), P("mp", None))
    out_specs = (P(rows_of, "mp"), P(rows_of, None), P("mp", None))
    return jax.shard_map(local, mesh=fine, in_specs=in_specs, out_specs=out_specs, check_vma=False)
```
